256 devices in a mesh: ctx: 32 (over y, z), head: 8 (over x, core).
Axes of the slice: x: 4, y: 4, z: 8, core: 2. Of those that a mesh axis runs over, the one named last changes fastest.
Arguments:
- lin_query: bfloat16 [65536, 3072], P('ctx', 'head'), may hold values from -6 to 6
- lin_key: bfloat16 [65536, 3072], P('ctx', 'head'), may hold values from -6 to 6
- lin_value: bfloat16 [65536, 3072], P('ctx', 'head'), may hold values from -6 to 6
- log_decay: float32 [24, 65536], P('head', 'ctx'), may hold values from -1 to 0, as said below
- norm_gain: float32 [3072], P('head'), may hold values from 0.25 to 1.75
- soft_query: bfloat16 [65536, 3072], P(('ctx', 'head')), may hold values from -12 to 12
- soft_key: bfloat16 [65536, 3072], P(('ctx', 'head')), may hold values from -12 to 12
- block_list: int32 [512, 16], P('ctx'), may hold values from -1 to 511, as said below
Outputs:
- lin_out: bfloat16 [65536, 3072], P('ctx', 'head')
- soft_out: bfloat16 [65536, 3072], P(('ctx', 'head'))
The draws below stay inside these ranges and needn't reach their ends.
Inputs may be any that keep to these rules, and one draw needn't show every extreme that they name: `block_list`: entry j of query block b is a key block from b - 32 to b, or -1 where that block would lie before the first; entry 0 is b itself, entry 1 is b - 32 (or -1); entries may repeat. `log_decay`: negative log decays.
All inputs are finite; a program needn't handle non-finite values.
Results may differ from the reference program's by a relative error of at most 0.0051.
Values may be sent and summed in bfloat16 or wider, within the bound.
A program may use at most 128 MiB of HBM per device.

```python
import math
import jax
import jax.numpy as jnp
from jax import lax

HEADS = 24
HD = 128
D = 3072
BLK = 128
NB = 16
TOK_CTX = 2048
TOKENS = 65536
NBLK = 512
REACH = 32


def draw_block_list(key, part):
    query_ids = jnp.arange(NBLK, dtype=jnp.int32)[:, None]
    extras = jax.random.randint(jax.random.fold_in(key, 11), (NBLK, NB - 2), 1, REACH + 1, dtype=jnp.int32)
    offsets = jnp.concatenate([jnp.zeros((NBLK, 1), jnp.int32), jnp.full((NBLK, 1), REACH, jnp.int32), extras], axis=1)
    targets = query_ids - offsets
    return jnp.where(targets >= 0, targets, -1).astype(jnp.int32)


def draw_log_decay(key, part):
    fast_share = 4
    head_picks = jax.random.randint(jax.random.fold_in(key, 31), (HEADS, 1), 0, 8)
    rapid_heads = head_picks < fast_share
    baseline_frequency = jnp.where(rapid_heads, 1.0 / 40.0, 0.3 / TOKENS)
    regions = jax.random.uniform(jax.random.fold_in(key, 32), (HEADS, TOKENS // TOK_CTX), minval=math.log(0.5), maxval=math.log(2.0))
    area_frequency = jnp.repeat(jnp.exp(regions), TOK_CTX, axis=1)
    random_perturbation = jax.random.uniform(jax.random.fold_in(key, 33), (HEADS, TOKENS), minval=0.5, maxval=1.5)
    location_list = jax.random.randint(jax.random.fold_in(key, 34), (2,), 0, TOKENS)
    token_locations = jnp.arange(TOKENS)
    spike_at_location = (token_locations == location_list[0]) | (token_locations == location_list[1])
    total_quantity = jax.random.uniform(jax.random.fold_in(key, 35), (HEADS, 1), minval=0.22, maxval=0.69)
    final_output = -(baseline_frequency * area_frequency * random_perturbation) - jnp.where(spike_at_location[None, :], total_quantity, 0.0)
    return final_output.astype(jnp.float32)


def soft_pair(key):
    base_query = jnp.clip(jax.random.normal(jax.random.fold_in(key, 21), (TOKENS, D)), -8.0, 8.0)
    base_key = jnp.clip(jax.random.normal(jax.random.fold_in(key, 22), (TOKENS, D)), -8.0, 8.0)
    return (base_query, base_key)


def draw_soft_query(key, part):
    return soft_pair(key)[0].astype(jnp.bfloat16)


def draw_soft_key(key, part):
    return soft_pair(key)[1].astype(jnp.bfloat16)


def levels(own_key, extent, cuts, smallest, largest):
    def one(dim, shards_of):
        draws = jax.random.uniform(jax.random.fold_in(jax.random.fold_in(own_key, 6), dim), (shards_of,), jnp.float32, smallest / len(cuts), largest / len(cuts))
        return jnp.repeat(jnp.exp(draws), extent[dim] // shards_of).reshape((-1,) + (1,) * (len(extent) - dim - 1))

    gain = one(*cuts[0])
    for cut in cuts[1:]:
        gain = gain * one(*cut)
    return gain


def bell_draw(own_key, shape, scale, most, pieces=(), held_as=jnp.bfloat16):
    gain = levels(own_key, shape, pieces, -0.22, 0.18) if pieces else 1.0
    drawn = jax.random.normal(own_key, shape, jnp.float32) * scale * gain
    return jnp.minimum(jnp.maximum(drawn, -most), most).astype(held_as)


def setup_inputs(seed: int = 0) -> dict:
    arg_keys = jax.random.split(jax.random.key(seed), 9)
    lin_query = bell_draw(arg_keys[0], (TOKENS, D), 1.0, 6.0, ((0, 32), (1, 8)))
    lin_key = bell_draw(arg_keys[1], (TOKENS, D), 1.0, 6.0, ((0, 32), (1, 8)))
    lin_value = bell_draw(arg_keys[2], (TOKENS, D), 1.0, 6.0, ((0, 32), (1, 8)))
    log_decay = draw_log_decay(jax.random.fold_in(arg_keys[8], 71), 0)
    norm_gain = jnp.clip(1.0 + 0.15 * jax.random.normal(arg_keys[4], (D,), jnp.float32), 0.25, 1.75)
    soft_query = draw_soft_query(jax.random.fold_in(arg_keys[8], 71), 0)
    soft_key = draw_soft_key(jax.random.fold_in(arg_keys[8], 71), 0)
    block_list = draw_block_list(jax.random.fold_in(arg_keys[8], 71), 0)
    return {"lin_query": lin_query, "lin_key": lin_key, "lin_value": lin_value, "log_decay": log_decay, "norm_gain": norm_gain, "soft_query": soft_query, "soft_key": soft_key, "block_list": block_list}


HIGHEST = lax.Precision.HIGHEST
EPSILON = 1e-06

def silu_round(inputs):
    values = inputs.astype(jnp.float32)
    return (values / (1.0 + jnp.exp(-values))).astype(jnp.bfloat16)

def lightning_part(lin_query, lin_key, lin_value, log_decay, norm_gain):

    def to_blocks(array):
        return array.reshape(NBLK, BLK, HEADS, HD).transpose(0, 2, 1, 3)
    feat_query = to_blocks(silu_round(lin_query))
    feat_key = to_blocks(silu_round(lin_key))
    values = to_blocks(lin_value)
    decays = log_decay.reshape(HEADS, NBLK, BLK).transpose(1, 0, 2)
    causal = jnp.arange(BLK)[:, None] >= jnp.arange(BLK)[None, :]
    gain_rows = norm_gain.reshape(HEADS, 1, HD)

    def advance(kv_state, inputs):
        block_query, block_key, block_value, block_decay = inputs
        running = jnp.cumsum(block_decay, axis=1)
        block_total = running[:, -1]
        query_f = block_query.astype(jnp.float32)
        key_f = block_key.astype(jnp.float32)
        value_f = block_value.astype(jnp.float32)
        scores = jnp.einsum('hte,hse->hts', query_f, key_f, precision=HIGHEST)
        spread = jnp.where(causal[None], running[:, :, None] - running[:, None, :], -1e+30)
        weights = (scores * jnp.exp(spread)).astype(jnp.bfloat16)
        intra_part = jnp.einsum('hts,hse->hte', weights.astype(jnp.float32), value_f, precision=HIGHEST)
        inter_part = jnp.einsum('hte,hef->htf', query_f * jnp.exp(running)[:, :, None], kv_state, precision=HIGHEST)
        scaled_key = key_f * jnp.exp(block_total[:, None] - running)[:, :, None]
        update = jnp.einsum('hse,hsf->hef', scaled_key, value_f, precision=HIGHEST)
        mixed = intra_part + inter_part
        mean_square = lax.optimization_barrier(jnp.mean(mixed * mixed, axis=-1, keepdims=True))
        normed = (mixed * lax.rsqrt(mean_square + EPSILON) * gain_rows).astype(jnp.bfloat16)
        return (jnp.exp(block_total)[:, None, None] * kv_state + update, normed)
    empty_state = jnp.zeros((HEADS, HD, HD), jnp.float32)
    _, outputs = lax.scan(advance, empty_state, (feat_query, feat_key, values, decays))
    return outputs.transpose(0, 2, 1, 3).reshape(TOKENS, D)

def softmax_part(soft_query, soft_key, soft_value, block_list):
    key_blocks = soft_key.reshape(NBLK, BLK, D)
    value_blocks = soft_value.reshape(NBLK, BLK, D)
    query_blocks = soft_query.reshape(NBLK, BLK, D)
    causal = jnp.arange(BLK)[:, None] >= jnp.arange(BLK)[None, :]
    earlier = jnp.arange(NB)[:, None] > jnp.arange(NB)[None, :]
    scale = HD ** (-0.5)

    def attend(inputs):
        query_block, listed, block_index = inputs
        repeat = jnp.any((listed[:, None] == listed[None, :]) & earlier, axis=1)
        usable = (listed >= 0) & jnp.logical_not(repeat)
        own_block = listed == block_index
        safe_index = jnp.maximum(listed, 0)
        keys_here = key_blocks[safe_index].reshape(NB, BLK, HEADS, HD).astype(jnp.float32)
        values_here = value_blocks[safe_index].reshape(NB, BLK, HEADS, HD).astype(jnp.float32)
        queries = query_block.reshape(BLK, HEADS, HD).astype(jnp.float32)
        logits = jnp.einsum('the,jshe->htjs', queries, keys_here, precision=HIGHEST) * scale
        allowed = usable[None, None, :, None] & (jnp.logical_not(own_block)[None, None, :, None] | causal[None, :, None, :])
        masked = jnp.where(allowed, logits, -jnp.inf)
        row_max = lax.optimization_barrier(jnp.max(masked, axis=(2, 3), keepdims=True))
        weights = jnp.exp(masked - row_max)
        row_total = lax.optimization_barrier(jnp.sum(weights, axis=(2, 3)))
        rounded = weights.astype(jnp.bfloat16).astype(jnp.float32)
        mixed = jnp.einsum('htjs,jshe->the', rounded, values_here, precision=HIGHEST)
        return (mixed / row_total.T[:, :, None]).astype(jnp.bfloat16).reshape(BLK, D)
    outputs = lax.map(attend, (query_blocks, block_list, jnp.arange(NBLK, dtype=jnp.int32)))
    return outputs.reshape(TOKENS, D)

def reference(lin_query, lin_key, lin_value, log_decay, norm_gain, soft_query, soft_key, block_list):
    lin_out = lightning_part(lin_query, lin_key, lin_value, log_decay, norm_gain)
    soft_out = softmax_part(soft_query, soft_key, lin_out, block_list)
    return (lin_out, soft_out)
```

```python
import functools
import math

import jax
import jax.numpy as jnp
from jax import lax
from jax.experimental import pallas as pl
from jax.experimental.pallas import tpu as pltpu
from jax.sharding import PartitionSpec as P

HD = 128
BLK = 128
NB = 16
EPSILON = 1e-06
MESH = pl.DeviceIdType.MESH
F32 = jnp.float32
BF16 = jnp.bfloat16
SCALE = HD ** (-0.5) * math.log2(math.e)
HIDDEN = -1e30
FLOOR = -1e20

NH = 3
HEADS = 8
ZS, YS = 8, 4
NCTX = ZS * YS
TOK = 2048
NBL = TOK // BLK
SUB = TOK // HEADS
WIDTH = NH * HD
PIECE = WIDTH // ZS
CHUNK = 512
PAIR = 2 * BLK
NPAIR = TOK // PAIR


def dot(a, b, ca=1, cb=0):
    return lax.dot_general(a, b, (((ca,), (cb,)), ((), ())), preferred_element_type=F32)


def silu(x):
    v = x.astype(F32)
    return (v / (1.0 + jnp.exp(-v))).astype(BF16)


def body(
    lq_any, lk_any, lv_any, cum_ref, gain_ref, sq_any, sk_any, bias_ref,
    lin_any, soft_any,
    lq, lk, lv, kb, upd, state, lin, vt,
    q0, q1, q2, kk, b1, b2,
    o2s, o1s, o2r, o1r, s2s, s1s, s2r, s1r, ost,
    e1s, e1r, e2r, e2s, e3s, inc,
    load_sem, own_sem, qs_sem, qr_sem, ks_sem, kr_sem, hop_s, hop_r, bias_s, bias_r,
    res_s, res_r, e1_s, e1_r, e2_s, e2_r, e3_s, e3_r, out_s, out_r, fin_sem,
):
    ctx = lax.axis_index("ctx")
    head = lax.axis_index("head")
    y, z = ctx // ZS, ctx % ZS
    prev = (ctx + NCTX - 1) % NCTX
    nxt = (ctx + 1) % NCTX

    def remote(src, dst, ss, rs, c, h):
        return pltpu.make_async_remote_copy(
            src_ref=src, dst_ref=dst, send_sem=ss, recv_sem=rs, device_id=(c, h), device_id_type=MESH
        )

    loads = [
        pltpu.make_async_copy(lk_any, lk, load_sem.at[0]),
        pltpu.make_async_copy(lv_any, lv, load_sem.at[1]),
        pltpu.make_async_copy(lq_any, lq, load_sem.at[2]),
    ]
    for c in loads:
        c.start()

    barrier = pltpu.get_barrier_semaphore()
    greeted = 0
    for o in range(1, HEADS):
        pl.semaphore_signal(barrier, inc=1, device_id=(ctx, (head + o) % HEADS), device_id_type=MESH)
        greeted += 1
    for o in range(1, ZS):
        pl.semaphore_signal(barrier, inc=1, device_id=(y * ZS + (z + o) % ZS, head), device_id_type=MESH)
        greeted += 1
    for o in range(1, YS):
        pl.semaphore_signal(barrier, inc=1, device_id=(((y + o) % YS) * ZS + z, head), device_id_type=MESH)
        greeted += 1
    for c in (prev, nxt):
        pl.semaphore_signal(barrier, inc=1, device_id=(c, head), device_id_type=MESH)
        greeted += 1
    pl.semaphore_wait(barrier, greeted)

    def regroup(src, dst, h, o, ss, rs):
        peer = (head + o) % HEADS
        col = pl.multiple_of(peer * WIDTH + h * HD, HD)
        row = pl.multiple_of(head * SUB, SUB)
        return remote(src.at[:, pl.ds(col, HD)], dst.at[h, pl.ds(row, SUB), :], ss.at[h, o], rs.at[h, o], ctx, peer)

    def own_part(src, dst, h, sem):
        col = pl.multiple_of(head * WIDTH + h * HD, HD)
        row = pl.multiple_of(head * SUB, SUB)
        return pltpu.make_async_copy(src.at[:, pl.ds(col, HD)], dst.at[h, pl.ds(row, SUB), :], sem)

    order = (1, 7, 2, 6, 3, 5, 4)
    for h in range(NH):
        own_part(sq_any, q0, h, own_sem.at[0, h]).start()
        for o in order:
            regroup(sq_any, q0, h, o, qs_sem, qr_sem).start()
    for h in range(NH):
        own_part(sk_any, kk, h, own_sem.at[1, h]).start()
        for o in order:
            regroup(sk_any, kk, h, o, ks_sem, kr_sem).start()

    bias_hop1 = remote(bias_ref.at[pl.ds(1, 2)], b1, bias_s.at[0], bias_r.at[0], prev, head)
    bias_hop2 = remote(b1.at[1], b2, bias_s.at[1], bias_r.at[1], prev, head)

    def hop1(h):
        return remote(q0.at[h], q1.at[h], hop_s.at[0, h], hop_r.at[0, h], prev, head)

    def hop2(h):
        return remote(q1.at[h], q2.at[h], hop_s.at[1, h], hop_r.at[1, h], prev, head)

    def start_hop1(h):
        own_part(sq_any, q0, h, own_sem.at[0, h]).wait()
        for o in order:
            regroup(sq_any, q0, h, o, qs_sem, qr_sem).wait_recv()
        hop1(h).start()

    def start_hop2(h):
        hop1(h).wait_recv()
        hop2(h).start()

    loads[0].wait()
    loads[1].wait()
    state[...] = jnp.zeros_like(state)

    def block_decay(h, n):
        row = cum_ref[h, pl.ds(n, 1), :]
        rowb = jnp.broadcast_to(row, (BLK, BLK))
        return row[:, BLK - 1 :], rowb, rowb.T

    def gather_state(n, carry):
        at = pl.multiple_of(n * BLK, BLK)
        for h in range(NH):
            total, _, colb = block_decay(h, n)
            key = silu(lk[pl.ds(at, BLK), h * HD : (h + 1) * HD])
            kb[h, pl.ds(at, BLK), :] = key
            value = lv[pl.ds(at, BLK), h * HD : (h + 1) * HD]
            weighted = key.astype(F32) * jnp.exp(total - colb)
            high = weighted.astype(BF16)
            low = (weighted - high.astype(F32)).astype(BF16)
            update = dot(high, value, 0, 0) + dot(low, value, 0, 0)
            upd[h, n] = update
            rows = slice(h * HD, (h + 1) * HD)
            state[rows, :] = jnp.exp(total) * state[rows, :] + update
        return carry

    lax.fori_loop(0, NBL // 2, gather_state, 0)
    start_hop1(0)
    bias_hop1.start()
    lax.fori_loop(NBL // 2, NBL, gather_state, 0)

    for h in range(NH):
        total = jnp.sum(cum_ref[h], axis=0, keepdims=True)[:, BLK - 1 :]
        e1s[:, PIECE + h, :] = jnp.broadcast_to(jnp.exp(total), (ZS, HD))
    for p in range(ZS):
        e1s[p, :PIECE, :] = state[p * PIECE : (p + 1) * PIECE, :]

    def e1_copy(o):
        peer = (z + o) % ZS
        return remote(e1s.at[peer], e1r.at[z], e1_s.at[o], e1_r.at[o], y * ZS + peer, head)

    def e2_copy(o):
        peer = (y + o) % YS
        return remote(e2s, e2r.at[y], e2_s.at[o], e2_r.at[o], peer * ZS + z, head)

    def e3_copy(o):
        peer = (z + o) % ZS
        rows = pl.ds(pl.multiple_of(z * PIECE, PIECE), PIECE)
        return remote(e3s.at[peer], inc.at[rows, :], e3_s.at[o], e3_r.at[o], y * ZS + peer, head)

    for o in range(1, ZS):
        e1_copy(o).start()
    start_hop1(1)
    e1r[z] = e1s[z]
    for o in range(1, ZS):
        e1_copy(o).wait_recv()
    place = z * PIECE + lax.broadcasted_iota(jnp.int32, (PIECE, HD), 0)
    acc = jnp.zeros((PIECE, HD), F32)
    reach = jnp.ones((PIECE, HD), F32)
    reaches = []
    for s in range(ZS):
        e3s[s] = acc
        reaches.append(reach)
        d = [e1r[s, PIECE + h : PIECE + h + 1, :] for h in range(NH)]
        step = jnp.where(place < HD, d[0], jnp.where(place < 2 * HD, d[1], d[2]))
        acc = step * acc + e1r[s, :PIECE, :]
        reach = reach * step
    e2s[:PIECE, :] = acc
    e2s[PIECE:, :] = reach
    for o in range(1, YS):
        e2_copy(o).start()
    start_hop1(2)
    e2r[y] = e2s[...]
    for o in range(1, YS):
        e2_copy(o).wait_recv()
    offset = jnp.zeros((PIECE, HD), F32)
    for s in range(YS):
        new = e2r[s, PIECE:, :] * offset + e2r[s, :PIECE, :]
        offset = jnp.where(s < y, new, offset)
    for s in range(ZS):
        e3s[s] = e3s[s] + reaches[s] * offset
    for o in range(1, ZS):
        e3_copy(o).start()
    inc[pl.ds(pl.multiple_of(z * PIECE, PIECE), PIECE), :] = e3s[z]
    loads[2].wait()
    for o in range(1, ZS):
        e3_copy(o).wait_recv()

    causal = lax.broadcasted_iota(jnp.int32, (BLK, BLK), 0) >= lax.broadcasted_iota(jnp.int32, (BLK, BLK), 1)

    def mix(h):
        gain = gain_ref[h : h + 1, :]

        def two(g, kv):
            for u in range(2):
                n = 2 * g + u
                at = pl.multiple_of(n * BLK, BLK)
                total, rowb, colb = block_decay(h, n)
                query = silu(lq[pl.ds(at, BLK), h * HD : (h + 1) * HD])
                key = kb[h, pl.ds(at, BLK), :]
                value = lv[pl.ds(at, BLK), h * HD : (h + 1) * HD]
                high = kv.astype(BF16)
                low = (kv - high.astype(F32)).astype(BF16)
                inter = jnp.exp(colb) * (dot(query, high) + dot(query, low))
                gap = jnp.where(causal, colb - rowb, HIDDEN)
                weights = (dot(query, key, 1, 1) * jnp.exp(gap)).astype(BF16)
                mixed = dot(weights, value) + inter
                square = jnp.mean(mixed * mixed, axis=-1, keepdims=True)
                normed = mixed * lax.rsqrt(square + EPSILON) * gain
                lin[h, pl.ds(at, BLK), :] = normed.astype(BF16)
                vt[h, :, pl.ds(at, BLK)] = normed.T.astype(BF16)
                kv = jnp.exp(total) * kv + upd[h, n]
            return kv

        lax.fori_loop(0, NBL // 2, two, inc[h * HD : (h + 1) * HD, :])
        store_lin(h).start()

    def store_lin(h):
        return pltpu.make_async_copy(lin.at[h], lin_any.at[:, pl.ds(h * HD, HD)], fin_sem.at[h])

    mix(0)
    start_hop2(0)
    bias_hop1.wait_recv()
    bias_hop2.start()
    mix(1)
    start_hop2(1)
    mix(2)

    key_row = lax.broadcasted_iota(jnp.int32, (CHUNK, PAIR), 0)
    query_lane = lax.broadcasted_iota(jnp.int32, (CHUNK, PAIR), 1)
    per = CHUNK // BLK

    def attend(h, queries, bias, role, finish):
        def pair_body(p, carry):
            lanes = pl.ds(pl.multiple_of(p * PAIR, PAIR), PAIR)
            query = queries[lanes, :]

            def step(c, state3, diagonal=False):
                m, l, acc = state3
                at = c * CHUNK if isinstance(c, int) else pl.multiple_of(c * CHUNK, CHUNK)
                logits = dot(kk[h, pl.ds(at, CHUNK), :], query, 1, 1)
                if diagonal:
                    logits = jnp.where(key_row + c * CHUNK <= query_lane + p * PAIR, logits, HIDDEN)
                parts = [logits[j * BLK : (j + 1) * BLK, :] for j in range(per)]
                pens = [bias[pl.ds(c * per + j, 1), lanes] for j in range(per)]
                new = m
                for part, pen in zip(parts, pens):
                    new = jnp.maximum(new, jnp.max(part, axis=0, keepdims=True) * SCALE + pen)
                keep = jnp.exp2(m - new)
                l = l * keep
                weights = []
                for part, pen in zip(parts, pens):
                    w = jnp.exp2(part * SCALE + (pen - new))
                    l = l + jnp.sum(w, axis=0, keepdims=True)
                    weights.append(w.astype(BF16))
                acc = acc * keep + dot(vt[h, :, pl.ds(at, CHUNK)], jnp.concatenate(weights, axis=0))
                return new, l, acc

            start = (
                jnp.full((1, PAIR), FLOOR, F32),
                jnp.zeros((1, PAIR), F32),
                jnp.zeros((HD, PAIR), F32),
            )
            if role == 1:
                result = start
                for c in range(TOK // CHUNK):
                    result = step(c, result)
            elif role == 2:
                result = lax.fori_loop(p // 2, TOK // CHUNK, step, start)
            else:
                result = lax.fori_loop(0, p // 2, step, start)
                result = step(p // 2, result, diagonal=True)
            finish(p, lanes, result)
            return carry

        lax.fori_loop(0, NPAIR, pair_body, 0)

    def merged(h, p, lanes, result, part, stats):
        m, l, acc = result
        m_in = stats[h, pl.ds(p, 1), :]
        l_in = stats[h, pl.ds(NPAIR + p, 1), :]
        new = jnp.maximum(m, m_in)
        mine, theirs = jnp.exp2(m - new), jnp.exp2(m_in - new)
        return new, l * mine + l_in * theirs, acc * mine + part[h, :, lanes].astype(F32) * theirs

    def store_part(h, p, lanes, result, part, stats):
        m, l, acc = result
        part[h, :, lanes] = acc.astype(BF16)
        stats[h, pl.ds(p, 1), :] = m
        stats[h, pl.ds(NPAIR + p, 1), :] = l

    def forward(h, role):
        o_s, o_r, s_s, s_r = (o2s, o2r, s2s, s2r) if role == 2 else (o1s, o1r, s1s, s1r)
        return (
            remote(o_s.at[h], o_r.at[h], res_s.at[role, 0, h], res_r.at[role, 0, h], nxt, head),
            remote(s_s.at[h], s_r.at[h], res_s.at[role, 1, h], res_r.at[role, 1, h], nxt, head),
        )

    def out_copy(h, o):
        peer = (head + o) % HEADS
        rows = pl.ds(pl.multiple_of(peer * SUB, SUB), SUB)
        col = pl.ds(pl.multiple_of(head * WIDTH + h * HD, HD), HD)
        return remote(ost.at[h, rows, :], soft_any.at[:, col], out_s.at[h, o], out_r.at[h, o], ctx, peer)

    def out_own(h):
        rows = pl.ds(pl.multiple_of(head * SUB, SUB), SUB)
        col = pl.ds(pl.multiple_of(head * WIDTH + h * HD, HD), HD)
        return pltpu.make_async_copy(ost.at[h, rows, :], soft_any.at[:, col], fin_sem.at[NH + h])

    def role2(h):
        hop2(h).wait_recv()
        attend(h, q2.at[h], b2, 2, lambda p, lanes, r: store_part(h, p, lanes, r, o2s, s2s))
        for c in forward(h, 2):
            c.start()

    def role1(h):
        for c in forward(h, 2):
            c.wait_recv()
        attend(
            h, q1.at[h], b1.at[0], 1,
            lambda p, lanes, r: store_part(h, p, lanes, merged(h, p, lanes, r, o2r, s2r), o1s, s1s),
        )
        for c in forward(h, 1):
            c.start()

    def role0(h):
        for c in forward(h, 1):
            c.wait_recv()

        def finish(p, lanes, r):
            m, l, acc = merged(h, p, lanes, r, o1r, s1r)
            ost[h, lanes, :] = (acc / l).T.astype(BF16)

        attend(h, q0.at[h], bias_ref.at[0], 0, finish)
        out_own(h).start()
        for o in order:
            out_copy(h, o).start()

    def keys_here(h):
        own_part(sk_any, kk, h, own_sem.at[1, h]).wait()
        for o in order:
            regroup(sk_any, kk, h, o, ks_sem, kr_sem).wait_recv()

    bias_hop2.wait_recv()
    keys_here(0)
    role2(0)
    start_hop2(2)
    keys_here(1)
    role2(1)
    role1(0)
    keys_here(2)
    role2(2)
    role1(1)
    role1(2)
    role0(0)
    role0(1)
    role0(2)

    for h in range(NH):
        store_lin(h).wait()
        out_own(h).wait()
        hop1(h).wait_send()
        hop2(h).wait_send()
        for role in (1, 2):
            for c in forward(h, role):
                c.wait_send()
        for o in order:
            regroup(sq_any, q0, h, o, qs_sem, qr_sem).wait_send()
            regroup(sk_any, kk, h, o, ks_sem, kr_sem).wait_send()
            out_copy(h, o).wait()
    bias_hop1.wait_send()
    bias_hop2.wait_send()
    for o in range(1, ZS):
        e1_copy(o).wait_send()
        e3_copy(o).wait_send()
    for o in range(1, YS):
        e2_copy(o).wait_send()


def shards(lin_query, lin_key, lin_value, log_decay, norm_gain, soft_query, soft_key, block_list):
    ctx = lax.axis_index("ctx")
    cumulated = jnp.cumsum(log_decay.reshape(NH, NBL, BLK), axis=2)
    ids = (ctx - jnp.arange(3, dtype=jnp.int32))[:, None] * NBL + jnp.arange(NBL, dtype=jnp.int32)[None, :]
    listed = jnp.any(block_list[None, None, :, :] == ids[:, :, None, None], axis=3) & (ids >= 0)[:, :, None]
    bias = jnp.repeat(jnp.where(listed, 0.0, HIDDEN).astype(F32), BLK, axis=2)
    anywhere = pl.BlockSpec(memory_space=pl.ANY)
    vmem = pl.BlockSpec(memory_space=pltpu.VMEM)
    dma = pltpu.SemaphoreType.DMA
    part = (NH, HD, TOK)
    rows = (NH, TOK, HD)
    stats = (NH, 2 * NPAIR, PAIR)
    return pl.pallas_call(
        body,
        out_shape=(
            jax.ShapeDtypeStruct((TOK, WIDTH), BF16),
            jax.ShapeDtypeStruct((SUB, HEADS * WIDTH), BF16),
        ),
        in_specs=[anywhere, anywhere, anywhere, vmem, vmem, anywhere, anywhere, vmem],
        out_specs=(anywhere, anywhere),
        scratch_shapes=[
            pltpu.VMEM((TOK, WIDTH), BF16),
            pltpu.VMEM((TOK, WIDTH), BF16),
            pltpu.VMEM((TOK, WIDTH), BF16),
            pltpu.VMEM(rows, BF16),
            pltpu.VMEM((NH, NBL, HD, HD), F32),
            pltpu.VMEM((WIDTH, HD), F32),
            pltpu.VMEM(rows, BF16),
            pltpu.VMEM(part, BF16),
            pltpu.VMEM(rows, BF16),
            pltpu.VMEM(rows, BF16),
            pltpu.VMEM(rows, BF16),
            pltpu.VMEM(rows, BF16),
            pltpu.VMEM((2, NBL, TOK), F32),
            pltpu.VMEM((NBL, TOK), F32),
            pltpu.VMEM(part, BF16),
            pltpu.VMEM(part, BF16),
            pltpu.VMEM(part, BF16),
            pltpu.VMEM(part, BF16),
            pltpu.VMEM(stats, F32),
            pltpu.VMEM(stats, F32),
            pltpu.VMEM(stats, F32),
            pltpu.VMEM(stats, F32),
            pltpu.VMEM(rows, BF16),
            pltpu.VMEM((ZS, PIECE + 8, HD), F32),
            pltpu.VMEM((ZS, PIECE + 8, HD), F32),
            pltpu.VMEM((YS, 2 * PIECE, HD), F32),
            pltpu.VMEM((2 * PIECE, HD), F32),
            pltpu.VMEM((ZS, PIECE, HD), F32),
            pltpu.VMEM((WIDTH, HD), F32),
            dma((3,)),
            dma((2, NH)),
            dma((NH, HEADS)),
            dma((NH, HEADS)),
            dma((NH, HEADS)),
            dma((NH, HEADS)),
            dma((2, NH)),
            dma((2, NH)),
            dma((2,)),
            dma((2,)),
            dma((3, 2, NH)),
            dma((3, 2, NH)),
            dma((ZS,)),
            dma((ZS,)),
            dma((YS,)),
            dma((YS,)),
            dma((ZS,)),
            dma((ZS,)),
            dma((NH, HEADS)),
            dma((NH, HEADS)),
            dma((2 * NH,)),
        ],
        compiler_params=pltpu.CompilerParams(
            collective_id=0, has_side_effects=True, vmem_limit_bytes=56 * 1024 * 1024
        ),
        cost_estimate=pl.CostEstimate(flops=20_000_000_000, bytes_accessed=12_000_000, transcendentals=30_000_000),
    )(
        lin_query, lin_key, lin_value, cumulated, norm_gain.reshape(NH, HD), soft_query, soft_key, bias
    )


def solution(mesh):
    placed = (
        P("ctx", "head"),
        P("ctx", "head"),
        P("ctx", "head"),
        P("head", "ctx"),
        P("head"),
        P(("ctx", "head"), None),
        P(("ctx", "head"), None),
        P("ctx", None),
    )
    return jax.shard_map(
        shards,
        mesh=mesh,
        in_specs=placed,
        out_specs=(P("ctx", "head"), P(("ctx", "head"), None)),
        check_vma=False,
    )
```

```python
import functools
import math

import jax
import jax.numpy as jnp
from jax import lax
from jax.experimental import pallas as pl
from jax.experimental.pallas import tpu as pltpu
from jax.sharding import PartitionSpec as P

HD = 128
BLK = 128
NB = 16
EPSILON = 1e-06
MESH = pl.DeviceIdType.MESH
F32 = jnp.float32
BF16 = jnp.bfloat16
SCALE = HD ** (-0.5) * math.log2(math.e)
HIDDEN = -1e30
FLOOR = -1e20

NH = 3
HEADS = 8
ZS, YS = 8, 4
NCTX = ZS * YS
TOK = 2048
NBL = TOK // BLK
SUB = TOK // HEADS
WIDTH = NH * HD
PIECE = WIDTH // ZS
PAIR = 2 * BLK
NPAIR = TOK // PAIR
HALF = TOK // 2
PARTS = 2 * NH
PPP = NPAIR // 2


def dot(a, b, ca=1, cb=0):
    return lax.dot_general(a, b, (((ca,), (cb,)), ((), ())), preferred_element_type=F32)


def silu(x):
    v = x.astype(F32)
    return (v / (1.0 + jnp.exp(-v))).astype(BF16)


def body(
    lq_any, lk_any, lv_any, decay_ref, gain_ref, sq_any, sk_any, list_ref,
    lin_any, soft_any,
    lq, lk, lv, kb, vraw, cum_ref, upd, state, lin, vt, acc0, acc1, st0, st1, b0, own_mask,
    q0, q1, q2, kk, b1, b2, far_mask, near_mask,
    o2s, o1s, o2r, o1r, s2s, s1s, s2r, s1r, ost,
    e1s, e1r, e2r, e2s, e3s, inc,
    load_sem, own_sem, qs_sem, qr_sem, ks_sem, kr_sem, hop_s, hop_r, bias_s, bias_r,
    res_s, res_r, e1_s, e1_r, e2_s, e2_r, e3_s, e3_r, out_s, out_r, fin_sem,
):
    ctx = lax.axis_index("ctx")
    head = lax.axis_index("head")
    y, z = ctx // ZS, ctx % ZS
    prev = (ctx + NCTX - 1) % NCTX
    nxt = (ctx + 1) % NCTX

    def remote(src, dst, ss, rs, c, h):
        return pltpu.make_async_remote_copy(
            src_ref=src, dst_ref=dst, send_sem=ss, recv_sem=rs, device_id=(c, h), device_id_type=MESH
        )

    loads = [
        pltpu.make_async_copy(lk_any, lk, load_sem.at[0]),
        pltpu.make_async_copy(lv_any, lv, load_sem.at[1]),
        pltpu.make_async_copy(lq_any, lq, load_sem.at[2]),
    ]
    for c in loads:
        c.start()

    barrier = pltpu.get_barrier_semaphore()
    greeted = 0
    for o in range(1, HEADS):
        pl.semaphore_signal(barrier, inc=1, device_id=(ctx, (head + o) % HEADS), device_id_type=MESH)
        greeted += 1
    for o in range(1, ZS):
        pl.semaphore_signal(barrier, inc=1, device_id=(y * ZS + (z + o) % ZS, head), device_id_type=MESH)
        greeted += 1
    for o in range(1, YS):
        pl.semaphore_signal(barrier, inc=1, device_id=(((y + o) % YS) * ZS + z, head), device_id_type=MESH)
        greeted += 1
    for c in (prev, nxt):
        pl.semaphore_signal(barrier, inc=1, device_id=(c, head), device_id_type=MESH)
        greeted += 1
    pl.semaphore_wait(barrier, greeted)

    def regroup(src, dst, h, o, ss, rs):
        peer = (head + o) % HEADS
        col = pl.multiple_of(peer * WIDTH + h * HD, HD)
        row = pl.multiple_of(head * SUB, SUB)
        return remote(src.at[:, pl.ds(col, HD)], dst.at[h, pl.ds(row, SUB), :], ss.at[h, o], rs.at[h, o], ctx, peer)

    def own_part(src, dst, h, sem):
        col = pl.multiple_of(head * WIDTH + h * HD, HD)
        row = pl.multiple_of(head * SUB, SUB)
        return pltpu.make_async_copy(src.at[:, pl.ds(col, HD)], dst.at[h, pl.ds(row, SUB), :], sem)

    order = (1, 7, 2, 6, 3, 5, 4)
    for h in range(NH):
        own_part(sq_any, q0, h, own_sem.at[0, h]).start()
        for o in order:
            regroup(sq_any, q0, h, o, qs_sem, qr_sem).start()
        own_part(sk_any, kk, h, own_sem.at[1, h]).start()
        for o in order:
            regroup(sk_any, kk, h, o, ks_sem, kr_sem).start()

    cum_ref[...] = jnp.zeros_like(cum_ref)
    for n in range(NBL):
        cum_ref[n, :NH, :] = decay_ref[:, n * BLK : (n + 1) * BLK]
    row_id = lax.broadcasted_iota(jnp.int32, (BLK, BLK), 0)
    lane_id = lax.broadcasted_iota(jnp.int32, (BLK, BLK), 1)
    until = (row_id <= lane_id).astype(F32).astype(BF16)
    rest = cum_ref[...].reshape(NBL * 8, BLK)
    total = jnp.zeros((NBL * 8, BLK), F32)
    for _ in range(3):
        part = rest.astype(BF16)
        total = total + dot(part, until)
        rest = rest - part.astype(F32)
    cum_ref[...] = total.reshape(NBL, 8, BLK)

    mask_hop1 = remote(own_mask, near_mask, bias_s.at[0], bias_r.at[0], prev, head)
    mask_hop2 = remote(near_mask.at[1], far_mask, bias_s.at[1], bias_r.at[1], prev, head)

    def hop1(c):
        h, half = c // 2, c % 2
        return remote(q0.at[h, pl.ds(half * HALF, HALF), :], q1.at[c], hop_s.at[0, c], hop_r.at[0, c], prev, head)

    def hop2(c):
        return remote(q1.at[c], q2.at[c], hop_s.at[1, c], hop_r.at[1, c], prev, head)

    def queries_here(h):
        own_part(sq_any, q0, h, own_sem.at[0, h]).wait()
        for o in order:
            regroup(sq_any, q0, h, o, qs_sem, qr_sem).wait_recv()

    def start_hop2(c):
        hop1(c).wait_recv()
        hop2(c).start()

    loads[0].wait()
    loads[1].wait()

    def gather_state(g, states):
        states = list(states)
        done = []
        for u in range(2):
            n = 2 * g + u
            at = pl.multiple_of(n * BLK, BLK)
            for h in range(NH):
                row = cum_ref[n, h : h + 1, :]
                end = row[:, BLK - 1 :]
                key = silu(lk[pl.ds(at, BLK), h * HD : (h + 1) * HD])
                value = lv[pl.ds(at, BLK), h * HD : (h + 1) * HD].T
                weighted = value.astype(F32) * jnp.exp(end - row)
                high = weighted.astype(BF16)
                low = (weighted - high.astype(F32)).astype(BF16)
                both = dot(jnp.concatenate([high, low], axis=0), key)
                update = both[:HD] + both[HD:]
                states[h] = jnp.exp(end) * states[h] + update
                done.append((h, n, at, key, value, update))
        for h, n, at, key, value, update in done:
            kb[h, pl.ds(at, BLK), :] = key
            vraw[h, :, pl.ds(at, BLK)] = value
            upd[h, n] = update
        return tuple(states)

    states = lax.fori_loop(0, NBL // 2, gather_state, tuple(jnp.zeros((HD, HD), F32) for _ in range(NH)))
    for h in range(NH):
        state[h * HD : (h + 1) * HD, :] = states[h]

    everything = jnp.sum(cum_ref[...], axis=0)[:, BLK - 1 :]
    for p in range(ZS):
        e1s[p, PIECE:, :] = jnp.broadcast_to(jnp.exp(everything), (8, HD))
    for p in range(ZS):
        e1s[p, :PIECE, :] = state[p * PIECE : (p + 1) * PIECE, :]

    def e1_copy(o):
        peer = (z + o) % ZS
        return remote(e1s.at[peer], e1r.at[z], e1_s.at[o], e1_r.at[o], y * ZS + peer, head)

    def e2_copy(o):
        peer = (y + o) % YS
        return remote(e2s, e2r.at[y], e2_s.at[o], e2_r.at[o], peer * ZS + z, head)

    def e3_copy(o):
        peer = (z + o) % ZS
        rows = pl.ds(pl.multiple_of(z * PIECE, PIECE), PIECE)
        return remote(e3s.at[peer], inc.at[rows, :], e3_s.at[o], e3_r.at[o], y * ZS + peer, head)

    for o in range(1, ZS):
        e1_copy(o).start()
    queries_here(0)
    hop1(0).start()
    e1r[z] = e1s[z]

    block_id = lax.broadcasted_iota(jnp.int32, (NBL, BLK), 0)
    block_lane = lax.broadcasted_iota(jnp.int32, (NBL, BLK), 1)
    for role in range(3):
        ids = block_id + (ctx - role) * NBL
        compact = jnp.full((NBL, BLK), HIDDEN, F32)
        for b in range(NBL):
            found = ids == list_ref[b, 0]
            for j in range(1, NB):
                found = found | (ids == list_ref[b, j])
            pen = jnp.where(found & (ids >= 0), 0.0, HIDDEN)
            if role == 0:
                b0[:, b * BLK : (b + 1) * BLK] = pen
            else:
                compact = jnp.where(block_lane == b, pen, compact)
        if role:
            own_mask[role - 1] = compact
    mask_hop1.start()

    def spread(mask, wide):
        for b in range(NBL):
            wide[:, b * BLK : (b + 1) * BLK] = jnp.broadcast_to(mask[:, b : b + 1], (NBL, BLK))

    for o in range(1, ZS):
        e1_copy(o).wait_recv()
    place = z * PIECE + lax.broadcasted_iota(jnp.int32, (PIECE, HD), 0)
    acc = jnp.zeros((PIECE, HD), F32)
    reach = jnp.ones((PIECE, HD), F32)
    reaches = []
    for s in range(ZS):
        e3s[s] = acc
        reaches.append(reach)
        d = [e1r[s, PIECE + h : PIECE + h + 1, :] for h in range(NH)]
        step = jnp.where(place < HD, d[0], jnp.where(place < 2 * HD, d[1], d[2]))
        acc = step * acc + e1r[s, :PIECE, :]
        reach = reach * step
    e2s[:PIECE, :] = acc
    e2s[PIECE:, :] = reach
    for o in range(1, YS):
        e2_copy(o).start()
    e2r[y] = e2s[...]
    for o in range(1, YS):
        e2_copy(o).wait_recv()
    offset = jnp.zeros((PIECE, HD), F32)
    for s in range(YS):
        new = e2r[s, PIECE:, :] * offset + e2r[s, :PIECE, :]
        offset = jnp.where(s < y, new, offset)
    for s in range(ZS):
        e3s[s] = e3s[s] + reaches[s] * offset
    for o in range(1, ZS):
        e3_copy(o).start()
    start_hop2(0)
    hop1(1).start()
    mask_hop1.wait_recv()
    mask_hop2.start()
    inc[pl.ds(pl.multiple_of(z * PIECE, PIECE), PIECE), :] = e3s[z]

    causal = row_id <= lane_id
    gains = [jnp.broadcast_to(gain_ref[:, h * HD : (h + 1) * HD], (BLK, HD)).T for h in range(NH)]

    def mix_head(h):
        def mix(g, state):
            done = []
            for u in range(4):
                n = 4 * g + u
                at = pl.multiple_of(n * BLK, BLK)
                row = cum_ref[n, h : h + 1, :]
                rowb = jnp.broadcast_to(row, (BLK, BLK))
                gap = jnp.where(causal, rowb - rowb.T, HIDDEN)
                query = silu(lq[pl.ds(at, BLK), h * HD : (h + 1) * HD])
                high = state.astype(BF16)
                low = (state - high.astype(F32)).astype(BF16)
                rows = jnp.concatenate([high, low, kb[h, pl.ds(at, BLK), :]], axis=0)
                products = dot(rows, query, 1, 1)
                weights = (products[2 * HD :] * jnp.exp(gap)).astype(BF16)
                mixed = dot(vraw[h, :, pl.ds(at, BLK)], weights)
                mixed = mixed + jnp.exp(row) * (products[:HD] + products[HD : 2 * HD])
                square = jnp.mean(mixed * mixed, axis=0, keepdims=True)
                normed = (mixed * lax.rsqrt(square + EPSILON) * gains[h]).astype(BF16)
                state = jnp.exp(row[:, BLK - 1 :]) * state + upd[h, n]
                done.append((at, normed))
            for at, normed in done:
                vt[h, :, pl.ds(at, BLK)] = normed
                lin[h, pl.ds(at, BLK), :] = normed.T
            return state

        lax.fori_loop(0, NBL // 4, mix, inc[h * HD : (h + 1) * HD, :])
        store_lin(h).start()

    def store_lin(h):
        return pltpu.make_async_copy(lin.at[h], lin_any.at[:, pl.ds(h * HD, HD)], fin_sem.at[h])

    pair_row = lax.broadcasted_iota(jnp.int32, (BLK, PAIR), 0)
    pair_lane = lax.broadcasted_iota(jnp.int32, (BLK, PAIR), 1)

    def score(h, queries, bias, role, p):
        lanes = slice(p * PAIR, (p + 1) * PAIR)
        lo, hi = ((0, 2 * p + 2), (0, NBL), (2 * p, NBL))[role]
        logits = dot(kk[h, lo * BLK : hi * BLK, :], queries(p), 1, 1)
        parts = [logits[j * BLK : (j + 1) * BLK, :] for j in range(hi - lo)]
        if role == 0:
            for u in range(2):
                parts[u - 2] = jnp.where(pair_row + u * BLK <= pair_lane, parts[u - 2], HIDDEN)
        pens = [bias[lo + j : lo + j + 1, lanes] for j in range(hi - lo)]
        top = jnp.full((1, PAIR), FLOOR, F32)
        for part, pen in zip(parts, pens):
            top = jnp.maximum(top, jnp.max(part, axis=0, keepdims=True) * SCALE + pen)
        return lo, hi, parts, pens, top

    def weigh(h, lo, hi, parts, pens, top):
        weights = []
        total = jnp.zeros((8, PAIR), F32)
        for part, pen in zip(parts, pens):
            w = jnp.exp2(part * SCALE + (pen - top))
            total = total + jnp.sum(w.reshape(BLK // 8, 8, PAIR), axis=0)
            weights.append(w.astype(BF16))
        acc = dot(vt[h, :, lo * BLK : hi * BLK], jnp.concatenate(weights, axis=0))
        return jnp.sum(total, axis=0, keepdims=True), acc

    def attend(c, queries, bias, role, out, stats):
        h, first = c // 2, (c % 2) * PPP
        waiting = []

        def finish():
            u, held = waiting.pop(0)
            l, acc = weigh(h, *held)
            out[c, :, u * PAIR : (u + 1) * PAIR] = acc.astype(out.dtype)
            stats[c, u : u + 1, :] = held[-1]
            stats[c, PPP + u : PPP + u + 1, :] = l

        for u in range(PPP):
            waiting.append((u, score(h, queries, bias, role, first + u)))
            if len(waiting) > 1:
                finish()
        finish()

    def merged(c, u, own, own_stats, part, stats):
        lanes = slice(u * PAIR, (u + 1) * PAIR)
        m, l = own_stats[c, u : u + 1, :], own_stats[c, PPP + u : PPP + u + 1, :]
        m_in, l_in = stats[c, u : u + 1, :], stats[c, PPP + u : PPP + u + 1, :]
        new = jnp.maximum(m, m_in)
        mine, theirs = jnp.exp2(m - new), jnp.exp2(m_in - new)
        acc = own[c, :, lanes] * mine + part[c, :, lanes].astype(F32) * theirs
        return new, l * mine + l_in * theirs, acc

    def forward(h, role):
        o_s, o_r, s_s, s_r = (o2s, o2r, s2s, s2r) if role == 2 else (o1s, o1r, s1s, s1r)
        return (
            remote(o_s.at[h], o_r.at[h], res_s.at[role, 0, h], res_r.at[role, 0, h], nxt, head),
            remote(s_s.at[h], s_r.at[h], res_s.at[role, 1, h], res_r.at[role, 1, h], nxt, head),
        )

    def out_region(h, sender):
        return soft_any.at[:, pl.ds(pl.multiple_of(sender * WIDTH + h * HD, HD), HD)]

    def out_copy(h, p, sender):
        rows = ost.at[h, pl.ds(p * SUB, SUB), :]
        return remote(rows, out_region(h, sender), out_s.at[h, p], out_r.at[h, sender], ctx, p)

    def out_own(h, p):
        return pltpu.make_async_copy(ost.at[h, pl.ds(p * SUB, SUB), :], out_region(h, head), fin_sem.at[NH + h])

    def far(c):
        hop2(c).wait_recv()
        attend(c, lambda p: q2[c, (p % PPP) * PAIR : (p % PPP + 1) * PAIR, :], b2, 2, o2s, s2s)
        for d in forward(c, 2):
            d.start()

    def near(c):
        attend(c, lambda p: q1[c, (p % PPP) * PAIR : (p % PPP + 1) * PAIR, :], b1, 1, acc1, st1)

    def own(c):
        attend(c, lambda p: q0[c // 2, p * PAIR : (p + 1) * PAIR, :], b0, 0, acc0, st0)

    def merge_near(c):
        for d in forward(c, 2):
            d.wait_recv()
        for u in range(PPP):
            m, l, acc = merged(c, u, acc1, st1, o2r, s2r)
            o1s[c, :, u * PAIR : (u + 1) * PAIR] = acc.astype(BF16)
            s1s[c, u : u + 1, :] = m
            s1s[c, PPP + u : PPP + u + 1, :] = l
        for d in forward(c, 1):
            d.start()

    def merge_own(c):
        for d in forward(c, 1):
            d.wait_recv()
        h = c // 2
        for u in range(PPP):
            p = (c % 2) * PPP + u
            m, l, acc = merged(c, u, acc0, st0, o1r, s1r)
            ost[h, p * PAIR : (p + 1) * PAIR, :] = (acc * (1.0 / l)).T.astype(BF16)

            @pl.when(head == p)
            def _():
                out_own(h, p).start()

            @pl.when(head != p)
            def _():
                out_copy(h, p, head).start()

    def keys_here(h):
        own_part(sk_any, kk, h, own_sem.at[1, h]).wait()
        for o in order:
            regroup(sk_any, kk, h, o, ks_sem, kr_sem).wait_recv()

    loads[2].wait()
    for o in range(1, ZS):
        e3_copy(o).wait_recv()
    mix_head(0)
    queries_here(1)
    hop1(2).start()
    spread(near_mask[0], b1)
    mask_hop2.wait_recv()
    spread(far_mask[...], b2)
    keys_here(0)
    far(0)
    start_hop2(1)
    hop1(3).start()
    mix_head(1)
    near(0)
    merge_near(0)
    start_hop2(2)
    queries_here(2)
    hop1(4).start()
    mix_head(2)
    own(0)
    far(1)
    near(1)
    own(1)
    start_hop2(3)
    hop1(5).start()
    merge_near(1)
    keys_here(1)
    far(2)
    near(2)
    merge_own(0)
    own(2)
    start_hop2(4)
    merge_near(2)
    far(3)
    near(3)
    start_hop2(5)
    merge_own(1)
    own(3)
    merge_near(3)
    keys_here(2)
    far(4)
    near(4)
    far(5)
    merge_own(2)
    own(4)
    merge_near(4)
    near(5)
    merge_near(5)
    merge_own(3)
    own(5)
    merge_own(4)
    merge_own(5)

    for h in range(NH):
        store_lin(h).wait()
        for o in order:
            regroup(sq_any, q0, h, o, qs_sem, qr_sem).wait_send()
            regroup(sk_any, kk, h, o, ks_sem, kr_sem).wait_send()
        for p in range(HEADS):

            @pl.when(head == p)
            def _():
                out_own(h, p).wait()

            @pl.when(head != p)
            def _():
                out_copy(h, p, head).wait_send()
                out_copy(h, p, p).wait_recv()
    for c in range(PARTS):
        hop1(c).wait_send()
        hop2(c).wait_send()
        for role in (1, 2):
            for d in forward(c, role):
                d.wait_send()
    mask_hop1.wait_send()
    mask_hop2.wait_send()
    for o in range(1, ZS):
        e1_copy(o).wait_send()
        e3_copy(o).wait_send()
    for o in range(1, YS):
        e2_copy(o).wait_send()


def shards(lin_query, lin_key, lin_value, log_decay, norm_gain, soft_query, soft_key, block_list):
    anywhere = pl.BlockSpec(memory_space=pl.ANY)
    vmem = pl.BlockSpec(memory_space=pltpu.VMEM)
    smem = pl.BlockSpec(memory_space=pltpu.SMEM)
    dma = pltpu.SemaphoreType.DMA
    wide = (NH, HD, TOK)
    part = (PARTS, HD, HALF)
    rows = (NH, TOK, HD)
    stats = (PARTS, 2 * PPP, PAIR)
    return pl.pallas_call(
        body,
        out_shape=(
            jax.ShapeDtypeStruct((TOK, WIDTH), BF16),
            jax.ShapeDtypeStruct((SUB, HEADS * WIDTH), BF16),
        ),
        in_specs=[anywhere, anywhere, anywhere, vmem, vmem, anywhere, anywhere, smem],
        out_specs=(anywhere, anywhere),
        scratch_shapes=[
            pltpu.VMEM((TOK, WIDTH), BF16),
            pltpu.VMEM((TOK, WIDTH), BF16),
            pltpu.VMEM((TOK, WIDTH), BF16),
            pltpu.VMEM(rows, BF16),
            pltpu.VMEM(wide, BF16),
            pltpu.VMEM((NBL, 8, BLK), F32),
            pltpu.VMEM((NH, NBL, HD, HD), F32),
            pltpu.VMEM((WIDTH, HD), F32),
            pltpu.VMEM(rows, BF16),
            pltpu.VMEM(wide, BF16),
            pltpu.VMEM(part, F32),
            pltpu.VMEM(part, F32),
            pltpu.VMEM(stats, F32),
            pltpu.VMEM(stats, F32),
            pltpu.VMEM((NBL, TOK), F32),
            pltpu.VMEM((2, NBL, BLK), F32),
            pltpu.VMEM(rows, BF16),
            pltpu.VMEM((PARTS, HALF, HD), BF16),
            pltpu.VMEM((PARTS, HALF, HD), BF16),
            pltpu.VMEM(rows, BF16),
            pltpu.VMEM((NBL, TOK), F32),
            pltpu.VMEM((NBL, TOK), F32),
            pltpu.VMEM((NBL, BLK), F32),
            pltpu.VMEM((2, NBL, BLK), F32),
            pltpu.VMEM(part, BF16),
            pltpu.VMEM(part, BF16),
            pltpu.VMEM(part, BF16),
            pltpu.VMEM(part, BF16),
            pltpu.VMEM(stats, F32),
            pltpu.VMEM(stats, F32),
            pltpu.VMEM(stats, F32),
            pltpu.VMEM(stats, F32),
            pltpu.VMEM(rows, BF16),
            pltpu.VMEM((ZS, PIECE + 8, HD), F32),
            pltpu.VMEM((ZS, PIECE + 8, HD), F32),
            pltpu.VMEM((YS, 2 * PIECE, HD), F32),
            pltpu.VMEM((2 * PIECE, HD), F32),
            pltpu.VMEM((ZS, PIECE, HD), F32),
            pltpu.VMEM((WIDTH, HD), F32),
            dma((3,)),
            dma((2, NH)),
            dma((NH, HEADS)),
            dma((NH, HEADS)),
            dma((NH, HEADS)),
            dma((NH, HEADS)),
            dma((2, PARTS)),
            dma((2, PARTS)),
            dma((2,)),
            dma((2,)),
            dma((3, 2, PARTS)),
            dma((3, 2, PARTS)),
            dma((ZS,)),
            dma((ZS,)),
            dma((YS,)),
            dma((YS,)),
            dma((ZS,)),
            dma((ZS,)),
            dma((NH, HEADS)),
            dma((NH, HEADS)),
            dma((2 * NH,)),
        ],
        compiler_params=pltpu.CompilerParams(
            collective_id=0, has_side_effects=True, vmem_limit_bytes=56 * 1024 * 1024
        ),
        cost_estimate=pl.CostEstimate(flops=20_000_000_000, bytes_accessed=12_000_000, transcendentals=30_000_000),
    )(
        lin_query, lin_key, lin_value, log_decay, norm_gain.reshape(1, WIDTH), soft_query, soft_key, block_list
    )


def solution(mesh):
    placed = (
        P("ctx", "head"),
        P("ctx", "head"),
        P("ctx", "head"),
        P("head", "ctx"),
        P("head"),
        P(("ctx", "head"), None),
        P(("ctx", "head"), None),
        P("ctx", None),
    )
    return jax.shard_map(
        shards,
        mesh=mesh,
        in_specs=placed,
        out_specs=(P("ctx", "head"), P(("ctx", "head"), None)),
        check_vma=False,
    )
```

```python
import functools
import math

import jax
import jax.numpy as jnp
from jax import lax
from jax.experimental import pallas as pl
from jax.experimental.pallas import tpu as pltpu
from jax.sharding import PartitionSpec as P

HD = 128
BLK = 128
NB = 16
EPSILON = 1e-06
UNROLL = 8
MESH = pl.DeviceIdType.MESH
F32 = jnp.float32
BF16 = jnp.bfloat16
SCALE = HD ** (-0.5) * math.log2(math.e)
HIDDEN = -1e30
FLOOR = -1e20

NH = 3
HEADS = 8
ZS, YS = 8, 4
NCTX = ZS * YS
TOK = 2048
NBL = TOK // BLK
SUB = TOK // HEADS
WIDTH = NH * HD
PIECE = WIDTH // ZS
PAIR = 2 * BLK
NPAIR = TOK // PAIR
SPLIT = 4
QUARTER = TOK // SPLIT
PPP = NPAIR // SPLIT
ORDER = [(h, q) for h in range(NH) for q in (range(SPLIT) if h == NH - 1 else range(SPLIT - 1, -1, -1))]
PARTS = len(ORDER)


def dot(a, b, ca=1, cb=0):
    return lax.dot_general(a, b, (((ca,), (cb,)), ((), ())), preferred_element_type=F32)


def silu(x):
    v = x.astype(F32)
    return (v / (1.0 + jnp.exp(-v))).astype(BF16)


def body(
    lq_any, lk_any, lv_any, decay_ref, gain_ref, sq_any, sk_any, list_ref,
    lin_any, soft_any,
    lq, lk, lv, kb, vraw, cum_ref, upd, state, lin, vt, acc0, acc1, st0, st1, b0, own_mask,
    q0, q1, q2, kk, b1, b2, far_mask, near_mask,
    o2s, o1s, o2r, o1r, s2s, s1s, s2r, s1r, ost,
    e1s, e1r, e2r, e2s, e3s, inc,
    load_sem, own_sem, qs_sem, qr_sem, ks_sem, kr_sem, hop_s, hop_r, bias_s, bias_r,
    res_s, res_r, e1_s, e1_r, e2_s, e2_r, e3_s, e3_r, out_s, out_r, fin_sem,
):
    ctx = lax.axis_index("ctx")
    head = lax.axis_index("head")
    y, z = ctx // ZS, ctx % ZS
    prev = (ctx + NCTX - 1) % NCTX
    nxt = (ctx + 1) % NCTX

    def remote(src, dst, ss, rs, c, h):
        return pltpu.make_async_remote_copy(
            src_ref=src, dst_ref=dst, send_sem=ss, recv_sem=rs, device_id=(c, h), device_id_type=MESH
        )

    loads = [
        pltpu.make_async_copy(lk_any, lk, load_sem.at[0]),
        pltpu.make_async_copy(lv_any, lv, load_sem.at[1]),
        pltpu.make_async_copy(lq_any, lq, load_sem.at[2]),
    ]
    for c in loads:
        c.start()

    barrier = pltpu.get_barrier_semaphore()
    greeted = 0
    for o in range(1, HEADS):
        pl.semaphore_signal(barrier, inc=1, device_id=(ctx, (head + o) % HEADS), device_id_type=MESH)
        greeted += 1
    for o in range(1, ZS):
        pl.semaphore_signal(barrier, inc=1, device_id=(y * ZS + (z + o) % ZS, head), device_id_type=MESH)
        greeted += 1
    for o in range(1, YS):
        pl.semaphore_signal(barrier, inc=1, device_id=(((y + o) % YS) * ZS + z, head), device_id_type=MESH)
        greeted += 1
    for c in (prev, nxt):
        pl.semaphore_signal(barrier, inc=1, device_id=(c, head), device_id_type=MESH)
        greeted += 1

    cum_ref[...] = jnp.zeros_like(cum_ref)
    for n in range(NBL):
        cum_ref[n, :NH, :] = decay_ref[:, n * BLK : (n + 1) * BLK]
    row_id = lax.broadcasted_iota(jnp.int32, (BLK, BLK), 0)
    lane_id = lax.broadcasted_iota(jnp.int32, (BLK, BLK), 1)
    until = (row_id <= lane_id).astype(F32).astype(BF16)
    rest = cum_ref[...].reshape(NBL * 8, BLK)
    total = jnp.zeros((NBL * 8, BLK), F32)
    for _ in range(3):
        part = rest.astype(BF16)
        total = total + dot(part, until)
        rest = rest - part.astype(F32)
    cum_ref[...] = total.reshape(NBL, 8, BLK)

    block_id = lax.broadcasted_iota(jnp.int32, (NBL, BLK), 0)
    block_lane = lax.broadcasted_iota(jnp.int32, (NBL, BLK), 1)
    for role in range(3):
        ids = block_id + (ctx - role) * NBL
        compact = jnp.full((NBL, BLK), HIDDEN, F32)
        for b in range(NBL):
            found = ids == list_ref[b, 0]
            for j in range(1, NB):
                found = found | (ids == list_ref[b, j])
            pen = jnp.where(found & (ids >= 0), 0.0, HIDDEN)
            if role == 0:
                b0[:, b * BLK : (b + 1) * BLK] = pen
            else:
                compact = jnp.where(block_lane == b, pen, compact)
        if role:
            own_mask[role - 1] = compact
    pl.semaphore_wait(barrier, greeted)

    def regroup(src, dst, h, o, ss, rs):
        peer = (head + o) % HEADS
        col = pl.multiple_of(peer * WIDTH + h * HD, HD)
        row = pl.multiple_of(head * SUB, SUB)
        return remote(src.at[:, pl.ds(col, HD)], dst.at[h, pl.ds(row, SUB), :], ss.at[h, o], rs.at[h, o], ctx, peer)

    def own_part(src, dst, h, sem):
        col = pl.multiple_of(head * WIDTH + h * HD, HD)
        row = pl.multiple_of(head * SUB, SUB)
        return pltpu.make_async_copy(src.at[:, pl.ds(col, HD)], dst.at[h, pl.ds(row, SUB), :], sem)

    order = (1, 7, 2, 6, 3, 5, 4)
    def start_regroup(h):
        own_part(sq_any, q0, h, own_sem.at[0, h]).start()
        for o in order:
            regroup(sq_any, q0, h, o, qs_sem, qr_sem).start()
        own_part(sk_any, kk, h, own_sem.at[1, h]).start()
        for o in order:
            regroup(sk_any, kk, h, o, ks_sem, kr_sem).start()

    start_regroup(0)
    mask_hop1 = remote(own_mask, near_mask, bias_s.at[0], bias_r.at[0], prev, head)
    mask_hop2 = remote(near_mask.at[1], far_mask, bias_s.at[1], bias_r.at[1], prev, head)

    def hop1(c):
        h, q = ORDER[c]
        return remote(q0.at[h, pl.ds(q * QUARTER, QUARTER), :], q1.at[c], hop_s.at[0, c], hop_r.at[0, c], prev, head)

    def hop2(c):
        return remote(q1.at[c], q2.at[c], hop_s.at[1, c], hop_r.at[1, c], prev, head)

    def queries_here(h):
        own_part(sq_any, q0, h, own_sem.at[0, h]).wait()
        for o in order:
            regroup(sq_any, q0, h, o, qs_sem, qr_sem).wait_recv()

    def start_hop2(c):
        hop1(c).wait_recv()
        hop2(c).start()

    mask_hop1.start()

    loads[0].wait()
    loads[1].wait()

    def gather_state(g, states):
        states = list(states)
        done = []
        for u in range(2):
            n = 2 * g + u
            at = pl.multiple_of(n * BLK, BLK)
            for h in range(NH):
                row = cum_ref[n, h : h + 1, :]
                end = row[:, BLK - 1 :]
                key = silu(lk[pl.ds(at, BLK), h * HD : (h + 1) * HD])
                value = lv[pl.ds(at, BLK), h * HD : (h + 1) * HD].T
                weighted = value.astype(F32) * jnp.exp(end - row)
                high = weighted.astype(BF16)
                low = (weighted - high.astype(F32)).astype(BF16)
                both = dot(jnp.concatenate([high, low], axis=0), key)
                update = both[:HD] + both[HD:]
                states[h] = jnp.exp(end) * states[h] + update
                done.append((h, n, at, key, value, update))
        for h, n, at, key, value, update in done:
            kb[h, pl.ds(at, BLK), :] = key
            vraw[h, :, pl.ds(at, BLK)] = value
            upd[h, n] = update
        return tuple(states)

    states = lax.fori_loop(0, NBL // 2, gather_state, tuple(jnp.zeros((HD, HD), F32) for _ in range(NH)))
    for h in range(NH):
        state[h * HD : (h + 1) * HD, :] = states[h]

    everything = jnp.sum(cum_ref[...], axis=0)[:, BLK - 1 :]
    decays = jnp.broadcast_to(jnp.exp(everything), (8, HD))
    coarse = decays.astype(BF16).astype(F32)
    tail = jnp.concatenate([coarse, decays - coarse], axis=0).astype(BF16)
    for p in range(ZS):
        e1s[p, :PIECE, :] = state[p * PIECE : (p + 1) * PIECE, :].astype(BF16)
        e1s[p, PIECE:, :] = tail

    def e1_copy(o):
        peer = (z + o) % ZS
        return remote(e1s.at[peer], e1r.at[z], e1_s.at[o], e1_r.at[o], y * ZS + peer, head)

    def e2_copy(o):
        peer = (y + o) % YS
        return remote(e2s, e2r.at[y], e2_s.at[o], e2_r.at[o], peer * ZS + z, head)

    def e3_copy(o):
        peer = (z + o) % ZS
        rows = pl.ds(pl.multiple_of(z * PIECE, PIECE), PIECE)
        return remote(e3s.at[peer], inc.at[rows, :], e3_s.at[o], e3_r.at[o], y * ZS + peer, head)

    for o in range(1, ZS):
        e1_copy(o).start()
    start_regroup(1)
    start_regroup(2)
    queries_here(0)
    hop1(0).start()
    hop1(1).start()
    e1r[z] = e1s[z]

    def spread(mask, wide):
        for b in range(NBL):
            wide[:, b * BLK : (b + 1) * BLK] = jnp.broadcast_to(mask[:, b : b + 1], (NBL, BLK))

    for o in range(1, ZS):
        e1_copy(o).wait_recv()
    place = z * PIECE + lax.broadcasted_iota(jnp.int32, (PIECE, HD), 0)
    acc = jnp.zeros((PIECE, HD), F32)
    reach = jnp.ones((PIECE, HD), F32)
    before, reaches = [], []
    for s in range(ZS):
        before.append(acc)
        reaches.append(reach)
        tail = e1r[s, PIECE:, :].astype(F32)
        d = [tail[h : h + 1] + tail[8 + h : 9 + h] for h in range(NH)]
        step = jnp.where(place < HD, d[0], jnp.where(place < 2 * HD, d[1], d[2]))
        acc = step * acc + e1r[s, :PIECE, :].astype(F32)
        reach = reach * step
    e2s[:PIECE, :] = acc
    e2s[PIECE:, :] = reach
    for o in range(1, YS):
        e2_copy(o).start()
    hop1(2).start()
    mask_hop1.wait_recv()
    mask_hop2.start()
    e2r[y] = e2s[...]
    for o in range(1, YS):
        e2_copy(o).wait_recv()
    offset = jnp.zeros((PIECE, HD), F32)
    for s in range(YS):
        new = e2r[s, PIECE:, :] * offset + e2r[s, :PIECE, :]
        offset = jnp.where(s < y, new, offset)
    for s in range(ZS):
        e3s[s] = (before[s] + reaches[s] * offset).astype(BF16)
    for o in range(1, ZS):
        e3_copy(o).start()
    start_hop2(0)
    start_hop2(1)
    hop1(3).start()
    inc[pl.ds(pl.multiple_of(z * PIECE, PIECE), PIECE), :] = e3s[z]

    causal = row_id <= lane_id
    gains = [jnp.broadcast_to(gain_ref[h * HD : (h + 1) * HD].reshape(1, HD), (BLK, HD)).T for h in range(NH)]

    def mix_head(h):
        def mix(g, state):
            done = []
            for u in range(UNROLL):
                n = UNROLL * g + u
                at = pl.multiple_of(n * BLK, BLK)
                row = cum_ref[n, h : h + 1, :]
                rowb = jnp.broadcast_to(row, (BLK, BLK))
                gap = jnp.where(causal, rowb - rowb.T, HIDDEN)
                query = silu(lq[pl.ds(at, BLK), h * HD : (h + 1) * HD])
                high = state.astype(BF16)
                low = (state - high.astype(F32)).astype(BF16)
                rows = jnp.concatenate([high, low, kb[h, pl.ds(at, BLK), :]], axis=0)
                products = dot(rows, query, 1, 1)
                weights = (products[2 * HD :] * jnp.exp(gap)).astype(BF16)
                mixed = dot(vraw[h, :, pl.ds(at, BLK)], weights)
                mixed = mixed + jnp.exp(row) * (products[:HD] + products[HD : 2 * HD])
                square = jnp.mean(mixed * mixed, axis=0, keepdims=True)
                normed = (mixed * lax.rsqrt(square + EPSILON) * gains[h]).astype(BF16)
                state = jnp.exp(row[:, BLK - 1 :]) * state + upd[h, n]
                done.append((at, normed))
            for at, normed in done:
                vt[h, :, pl.ds(at, BLK)] = normed
                lin[pl.ds(at, BLK), h * HD : (h + 1) * HD] = normed.T
            return state

        lax.fori_loop(0, NBL // UNROLL, mix, inc[h * HD : (h + 1) * HD, :].astype(F32))
        store_lin(h).start()

    def store_lin(h):
        cols = slice(h * HD, (h + 1) * HD)
        return pltpu.make_async_copy(lin.at[:, cols], lin_any.at[:, cols], fin_sem.at[h])

    pair_row = lax.broadcasted_iota(jnp.int32, (BLK, PAIR), 0)
    pair_lane = lax.broadcasted_iota(jnp.int32, (BLK, PAIR), 1)

    def score(h, queries, bias, role, p):
        lanes = slice(p * PAIR, (p + 1) * PAIR)
        lo, hi = ((0, 2 * p + 2), (0, NBL), (2 * p, NBL))[role]
        logits = dot(kk[h, lo * BLK : hi * BLK, :], queries(p), 1, 1)
        parts = [logits[j * BLK : (j + 1) * BLK, :] for j in range(hi - lo)]
        if role == 0:
            for u in range(2):
                parts[u - 2] = jnp.where(pair_row + u * BLK <= pair_lane, parts[u - 2], HIDDEN)
        pens = [bias[lo + j : lo + j + 1, lanes] for j in range(hi - lo)]
        top = jnp.full((1, PAIR), FLOOR, F32)
        for part, pen in zip(parts, pens):
            top = jnp.maximum(top, jnp.max(part, axis=0, keepdims=True) * SCALE + pen)
        return lo, hi, parts, pens, top

    def weigh(h, lo, hi, parts, pens, top):
        weights = []
        total = jnp.zeros((8, PAIR), F32)
        for part, pen in zip(parts, pens):
            w = jnp.exp2(part * SCALE + (pen - top))
            total = total + jnp.sum(w.reshape(BLK // 8, 8, PAIR), axis=0)
            weights.append(w.astype(BF16))
        acc = dot(vt[h, :, lo * BLK : hi * BLK], jnp.concatenate(weights, axis=0))
        return jnp.sum(total, axis=0, keepdims=True), acc

    def attend(c, queries, bias, role, out, stats):
        h, first = ORDER[c][0], ORDER[c][1] * PPP
        waiting = []

        def finish():
            u, held = waiting.pop(0)
            l, acc = weigh(h, *held)
            out[c, :, u * PAIR : (u + 1) * PAIR] = acc.astype(out.dtype)
            stats[c, u : u + 1, :] = held[-1]
            stats[c, PPP + u : PPP + u + 1, :] = l

        for u in range(PPP):
            waiting.append((u, score(h, queries, bias, role, first + u)))
            if len(waiting) > 1:
                finish()
        finish()

    def merged(c, u, own, own_stats, part, stats):
        lanes = slice(u * PAIR, (u + 1) * PAIR)
        m, l = own_stats[c, u : u + 1, :], own_stats[c, PPP + u : PPP + u + 1, :]
        m_in, l_in = stats[c, u : u + 1, :], stats[c, PPP + u : PPP + u + 1, :]
        new = jnp.maximum(m, m_in)
        mine, theirs = jnp.exp2(m - new), jnp.exp2(m_in - new)
        acc = own[c, :, lanes] * mine + part[c, :, lanes].astype(F32) * theirs
        return new, l * mine + l_in * theirs, acc

    def forward(h, role):
        o_s, o_r, s_s, s_r = (o2s, o2r, s2s, s2r) if role == 2 else (o1s, o1r, s1s, s1r)
        return (
            remote(o_s.at[h], o_r.at[h], res_s.at[role, 0, h], res_r.at[role, 0, h], nxt, head),
            remote(s_s.at[h], s_r.at[h], res_s.at[role, 1, h], res_r.at[role, 1, h], nxt, head),
        )

    def out_region(h, sender):
        return soft_any.at[:, pl.ds(pl.multiple_of(sender * WIDTH + h * HD, HD), HD)]

    def out_copy(h, p, sender):
        rows = ost.at[h, pl.ds(p * SUB, SUB), :]
        return remote(rows, out_region(h, sender), out_s.at[h, p], out_r.at[h, sender], ctx, p)

    def out_own(h, p):
        return pltpu.make_async_copy(ost.at[h, pl.ds(p * SUB, SUB), :], out_region(h, head), fin_sem.at[NH + h])

    def far(c):
        hop2(c).wait_recv()
        attend(c, lambda p: q2[c, (p % PPP) * PAIR : (p % PPP + 1) * PAIR, :], b2, 2, o2s, s2s)
        for d in forward(c, 2):
            d.start()

    def near(c):
        attend(c, lambda p: q1[c, (p % PPP) * PAIR : (p % PPP + 1) * PAIR, :], b1, 1, acc1, st1)

    def own(c):
        attend(c, lambda p: q0[ORDER[c][0], p * PAIR : (p + 1) * PAIR, :], b0, 0, acc0, st0)

    def merge_near(c):
        for d in forward(c, 2):
            d.wait_recv()
        for u in range(PPP):
            m, l, acc = merged(c, u, acc1, st1, o2r, s2r)
            o1s[c, :, u * PAIR : (u + 1) * PAIR] = acc.astype(BF16)
            s1s[c, u : u + 1, :] = m
            s1s[c, PPP + u : PPP + u + 1, :] = l
        for d in forward(c, 1):
            d.start()

    def merge_own(c):
        for d in forward(c, 1):
            d.wait_recv()
        h = ORDER[c][0]
        for u in range(PPP):
            p = ORDER[c][1] * PPP + u
            m, l, acc = merged(c, u, acc0, st0, o1r, s1r)
            ost[h, p * PAIR : (p + 1) * PAIR, :] = (acc * (1.0 / l)).T.astype(BF16)

            @pl.when(head == p)
            def _():
                out_own(h, p).start()

            @pl.when(head != p)
            def _():
                out_copy(h, p, head).start()

    def keys_here(h):
        own_part(sk_any, kk, h, own_sem.at[1, h]).wait()
        for o in order:
            regroup(sk_any, kk, h, o, ks_sem, kr_sem).wait_recv()

    loads[2].wait()
    for o in range(1, ZS):
        e3_copy(o).wait_recv()
    mix_head(0)
    spread(near_mask[0], b1)
    mask_hop2.wait_recv()
    spread(far_mask[...], b2)
    for c in range(PARTS):
        if c + 2 < PARTS:
            start_hop2(c + 2)
        if c + 4 < PARTS:
            if (c + 4) % SPLIT == 0:
                queries_here((c + 4) // SPLIT)
            hop1(c + 4).start()
        if c % SPLIT == 0:
            keys_here(c // SPLIT)
        far(c)
        near(c)
        if c >= 1:
            merge_near(c - 1)
        own(c)
        if c >= 2:
            merge_own(c - 2)
        if c in (1, 4):
            mix_head(1 if c == 1 else 2)
    merge_near(PARTS - 1)
    merge_own(PARTS - 2)
    merge_own(PARTS - 1)

    for h in range(NH):
        store_lin(h).wait()
        for o in order:
            regroup(sq_any, q0, h, o, qs_sem, qr_sem).wait_send()
            regroup(sk_any, kk, h, o, ks_sem, kr_sem).wait_send()
        for p in range(HEADS):

            @pl.when(head == p)
            def _():
                out_own(h, p).wait()

            @pl.when(head != p)
            def _():
                out_copy(h, p, head).wait_send()
                out_copy(h, p, p).wait_recv()
    for c in range(PARTS):
        hop1(c).wait_send()
        hop2(c).wait_send()
        for role in (1, 2):
            for d in forward(c, role):
                d.wait_send()
    mask_hop1.wait_send()
    mask_hop2.wait_send()
    for o in range(1, ZS):
        e1_copy(o).wait_send()
        e3_copy(o).wait_send()
    for o in range(1, YS):
        e2_copy(o).wait_send()


def shards(lin_query, lin_key, lin_value, log_decay, norm_gain, soft_query, soft_key, block_list):
    anywhere = pl.BlockSpec(memory_space=pl.ANY)
    vmem = pl.BlockSpec(memory_space=pltpu.VMEM)
    smem = pl.BlockSpec(memory_space=pltpu.SMEM)
    dma = pltpu.SemaphoreType.DMA
    wide = (NH, HD, TOK)
    part = (PARTS, HD, QUARTER)
    rows = (NH, TOK, HD)
    stats = (PARTS, 2 * PPP, PAIR)
    return pl.pallas_call(
        body,
        out_shape=(
            jax.ShapeDtypeStruct((TOK, WIDTH), BF16),
            jax.ShapeDtypeStruct((SUB, HEADS * WIDTH), BF16),
        ),
        in_specs=[anywhere, anywhere, anywhere, vmem, vmem, anywhere, anywhere, smem],
        out_specs=(anywhere, anywhere),
        scratch_shapes=[
            pltpu.VMEM((TOK, WIDTH), BF16),
            pltpu.VMEM((TOK, WIDTH), BF16),
            pltpu.VMEM((TOK, WIDTH), BF16),
            pltpu.VMEM(rows, BF16),
            pltpu.VMEM(wide, BF16),
            pltpu.VMEM((NBL, 8, BLK), F32),
            pltpu.VMEM((NH, NBL, HD, HD), F32),
            pltpu.VMEM((WIDTH, HD), F32),
            pltpu.VMEM((TOK, WIDTH), BF16),
            pltpu.VMEM(wide, BF16),
            pltpu.VMEM(part, F32),
            pltpu.VMEM(part, F32),
            pltpu.VMEM(stats, F32),
            pltpu.VMEM(stats, F32),
            pltpu.VMEM((NBL, TOK), F32),
            pltpu.VMEM((2, NBL, BLK), F32),
            pltpu.VMEM(rows, BF16),
            pltpu.VMEM((PARTS, QUARTER, HD), BF16),
            pltpu.VMEM((PARTS, QUARTER, HD), BF16),
            pltpu.VMEM(rows, BF16),
            pltpu.VMEM((NBL, TOK), F32),
            pltpu.VMEM((NBL, TOK), F32),
            pltpu.VMEM((NBL, BLK), F32),
            pltpu.VMEM((2, NBL, BLK), F32),
            pltpu.VMEM(part, BF16),
            pltpu.VMEM(part, BF16),
            pltpu.VMEM(part, BF16),
            pltpu.VMEM(part, BF16),
            pltpu.VMEM(stats, F32),
            pltpu.VMEM(stats, F32),
            pltpu.VMEM(stats, F32),
            pltpu.VMEM(stats, F32),
            pltpu.VMEM(rows, BF16),
            pltpu.VMEM((ZS, PIECE + 16, HD), BF16),
            pltpu.VMEM((ZS, PIECE + 16, HD), BF16),
            pltpu.VMEM((YS, 2 * PIECE, HD), F32),
            pltpu.VMEM((2 * PIECE, HD), F32),
            pltpu.VMEM((ZS, PIECE, HD), BF16),
            pltpu.VMEM((WIDTH, HD), BF16),
            dma((3,)),
            dma((2, NH)),
            dma((NH, HEADS)),
            dma((NH, HEADS)),
            dma((NH, HEADS)),
            dma((NH, HEADS)),
            dma((2, PARTS)),
            dma((2, PARTS)),
            dma((2,)),
            dma((2,)),
            dma((3, 2, PARTS)),
            dma((3, 2, PARTS)),
            dma((ZS,)),
            dma((ZS,)),
            dma((YS,)),
            dma((YS,)),
            dma((ZS,)),
            dma((ZS,)),
            dma((NH, HEADS)),
            dma((NH, HEADS)),
            dma((2 * NH,)),
        ],
        compiler_params=pltpu.CompilerParams(
            collective_id=0, has_side_effects=True, vmem_limit_bytes=56 * 1024 * 1024
        ),
        cost_estimate=pl.CostEstimate(flops=20_000_000_000, bytes_accessed=12_000_000, transcendentals=30_000_000),
    )(
        lin_query, lin_key, lin_value, log_decay, norm_gain, soft_query, soft_key, block_list
    )


def solution(mesh):
    placed = (
        P("ctx", "head"),
        P("ctx", "head"),
        P("ctx", "head"),
        P("head", "ctx"),
        P("head"),
        P(("ctx", "head"), None),
        P(("ctx", "head"), None),
        P("ctx", None),
    )
    return jax.shard_map(
        shards,
        mesh=mesh,
        in_specs=placed,
        out_specs=(P("ctx", "head"), P(("ctx", "head"), None)),
        check_vma=False,
    )
```

```python
import functools
import math

import jax
import jax.numpy as jnp
from jax import lax
from jax.experimental import pallas as pl
from jax.experimental.pallas import tpu as pltpu
from jax.sharding import PartitionSpec as P

HD = 128
BLK = 128
NB = 16
EPSILON = 1e-06
UNROLL = 8
MESH = pl.DeviceIdType.MESH
F32 = jnp.float32
BF16 = jnp.bfloat16
SCALE = HD ** (-0.5) * math.log2(math.e)
HIDDEN = -1e30
FLOOR = -1e20

NH = 3
HEADS = 8
ZS, YS = 8, 4
NCTX = ZS * YS
TOK = 2048
NBL = TOK // BLK
SUB = TOK // HEADS
WIDTH = NH * HD
PIECE = WIDTH // ZS
PAIR = 2 * BLK
NPAIR = TOK // PAIR
SPLIT = 4
QUARTER = TOK // SPLIT
PPP = NPAIR // SPLIT
ORDER = [(h, q) for h in range(NH) for q in (range(SPLIT) if h == NH - 1 else range(SPLIT - 1, -1, -1))]
PARTS = len(ORDER)


def dot(a, b, ca=1, cb=0):
    return lax.dot_general(a, b, (((ca,), (cb,)), ((), ())), preferred_element_type=F32)


def silu(x):
    v = x.astype(F32)
    return (v / (1.0 + jnp.exp(-v))).astype(BF16)


def body(
    lq_any, lk_any, lv_any, decay_ref, gain_ref, sq_any, sk_any, list_ref,
    lin_any, soft_any,
    lq, lk, lv, kb, vraw, cum_ref, upd, state, within, lin, vt, acc0, acc1, st0, st1, b0, own_mask,
    q0, q1, q2, kk, b1, b2, far_mask, near_mask,
    o2s, o1s, o2r, o1r, s2s, s1s, s2r, s1r, ost,
    e1s, e1r, e2r, e2s, e3s, inc,
    load_sem, own_sem, qs_sem, qr_sem, ks_sem, kr_sem, hop_s, hop_r, bias_s, bias_r,
    res_s, res_r, e1_s, e1_r, e2_s, e2_r, e3_s, e3_r, out_s, out_r, fin_sem,
):
    ctx = lax.axis_index("ctx")
    head = lax.axis_index("head")
    y, z = ctx // ZS, ctx % ZS
    prev = (ctx + NCTX - 1) % NCTX
    nxt = (ctx + 1) % NCTX

    def remote(src, dst, ss, rs, c, h):
        return pltpu.make_async_remote_copy(
            src_ref=src, dst_ref=dst, send_sem=ss, recv_sem=rs, device_id=(c, h), device_id_type=MESH
        )

    loads = [
        pltpu.make_async_copy(lk_any, lk, load_sem.at[0]),
        pltpu.make_async_copy(lv_any, lv, load_sem.at[1]),
        pltpu.make_async_copy(lq_any, lq, load_sem.at[2]),
    ]
    for c in loads:
        c.start()

    barrier = pltpu.get_barrier_semaphore()
    greeted = 0
    for o in range(1, HEADS):
        pl.semaphore_signal(barrier, inc=1, device_id=(ctx, (head + o) % HEADS), device_id_type=MESH)
        greeted += 1
    for o in range(1, ZS):
        pl.semaphore_signal(barrier, inc=1, device_id=(y * ZS + (z + o) % ZS, head), device_id_type=MESH)
        greeted += 1
    for o in range(1, YS):
        pl.semaphore_signal(barrier, inc=1, device_id=(((y + o) % YS) * ZS + z, head), device_id_type=MESH)
        greeted += 1
    for c in (prev, nxt):
        pl.semaphore_signal(barrier, inc=1, device_id=(c, head), device_id_type=MESH)
        greeted += 1

    cum_ref[...] = jnp.zeros_like(cum_ref)
    for n in range(NBL):
        cum_ref[n, :NH, :] = decay_ref[:, n * BLK : (n + 1) * BLK]
    row_id = lax.broadcasted_iota(jnp.int32, (BLK, BLK), 0)
    lane_id = lax.broadcasted_iota(jnp.int32, (BLK, BLK), 1)
    until = (row_id <= lane_id).astype(F32).astype(BF16)
    rest = cum_ref[...].reshape(NBL * 8, BLK)
    total = jnp.zeros((NBL * 8, BLK), F32)
    for _ in range(3):
        part = rest.astype(BF16)
        total = total + dot(part, until)
        rest = rest - part.astype(F32)
    cum_ref[...] = total.reshape(NBL, 8, BLK)

    block_id = lax.broadcasted_iota(jnp.int32, (NBL, BLK), 0)
    block_lane = lax.broadcasted_iota(jnp.int32, (NBL, BLK), 1)
    for role in range(3):
        ids = block_id + (ctx - role) * NBL
        compact = jnp.full((NBL, BLK), HIDDEN, F32)
        for b in range(NBL):
            found = ids == list_ref[b, 0]
            for j in range(1, NB):
                found = found | (ids == list_ref[b, j])
            pen = jnp.where(found & (ids >= 0), 0.0, HIDDEN)
            if role == 0:
                b0[:, b * BLK : (b + 1) * BLK] = pen
            else:
                compact = jnp.where(block_lane == b, pen, compact)
        if role:
            own_mask[role - 1] = compact
    pl.semaphore_wait(barrier, greeted)

    def regroup(src, dst, h, o, ss, rs):
        peer = (head + o) % HEADS
        col = pl.multiple_of(peer * WIDTH + h * HD, HD)
        row = pl.multiple_of(head * SUB, SUB)
        return remote(src.at[:, pl.ds(col, HD)], dst.at[h, pl.ds(row, SUB), :], ss.at[h, o], rs.at[h, o], ctx, peer)

    def own_part(src, dst, h, sem):
        col = pl.multiple_of(head * WIDTH + h * HD, HD)
        row = pl.multiple_of(head * SUB, SUB)
        return pltpu.make_async_copy(src.at[:, pl.ds(col, HD)], dst.at[h, pl.ds(row, SUB), :], sem)

    order = (1, 7, 2, 6, 3, 5, 4)
    def start_regroup(h):
        own_part(sq_any, q0, h, own_sem.at[0, h]).start()
        for o in order:
            regroup(sq_any, q0, h, o, qs_sem, qr_sem).start()
        own_part(sk_any, kk, h, own_sem.at[1, h]).start()
        for o in order:
            regroup(sk_any, kk, h, o, ks_sem, kr_sem).start()

    start_regroup(0)
    mask_hop1 = remote(own_mask, near_mask, bias_s.at[0], bias_r.at[0], prev, head)
    mask_hop2 = remote(near_mask.at[1], far_mask, bias_s.at[1], bias_r.at[1], prev, head)

    def hop1(c):
        h, q = ORDER[c]
        return remote(q0.at[h, pl.ds(q * QUARTER, QUARTER), :], q1.at[c], hop_s.at[0, c], hop_r.at[0, c], prev, head)

    def hop2(c):
        return remote(q1.at[c], q2.at[c], hop_s.at[1, c], hop_r.at[1, c], prev, head)

    def queries_here(h):
        own_part(sq_any, q0, h, own_sem.at[0, h]).wait()
        for o in order:
            regroup(sq_any, q0, h, o, qs_sem, qr_sem).wait_recv()

    def start_hop2(c):
        hop1(c).wait_recv()
        hop2(c).start()

    mask_hop1.start()

    loads[0].wait()
    loads[1].wait()

    def gather_state(g, states):
        states = list(states)
        done = []
        for u in range(2):
            n = 2 * g + u
            at = pl.multiple_of(n * BLK, BLK)
            for h in range(NH):
                row = cum_ref[n, h : h + 1, :]
                end = row[:, BLK - 1 :]
                key = silu(lk[pl.ds(at, BLK), h * HD : (h + 1) * HD])
                value = lv[pl.ds(at, BLK), h * HD : (h + 1) * HD].T
                weighted = value.astype(F32) * jnp.exp(end - row)
                high = weighted.astype(BF16)
                low = (weighted - high.astype(F32)).astype(BF16)
                both = dot(jnp.concatenate([high, low], axis=0), key)
                update = both[:HD] + both[HD:]
                states[h] = jnp.exp(end) * states[h] + update
                done.append((h, n, at, key, value, update))
        for h, n, at, key, value, update in done:
            kb[h, pl.ds(at, BLK), :] = key
            vraw[h, :, pl.ds(at, BLK)] = value
            upd[h, n] = update
        return tuple(states)

    states = lax.fori_loop(0, NBL // 2, gather_state, tuple(jnp.zeros((HD, HD), F32) for _ in range(NH)))
    for h in range(NH):
        state[h * HD : (h + 1) * HD, :] = states[h]

    everything = jnp.sum(cum_ref[...], axis=0)[:, BLK - 1 :]
    decays = jnp.broadcast_to(jnp.exp(everything), (8, HD))
    coarse = decays.astype(BF16).astype(F32)
    tail = jnp.concatenate([coarse, decays - coarse], axis=0).astype(BF16)
    for p in range(ZS):
        e1s[p, :PIECE, :] = state[p * PIECE : (p + 1) * PIECE, :].astype(BF16)
        e1s[p, PIECE:, :] = tail

    def e1_copy(o):
        peer = (z + o) % ZS
        return remote(e1s.at[peer], e1r.at[z], e1_s.at[o], e1_r.at[o], y * ZS + peer, head)

    def e2_copy(o):
        peer = (y + o) % YS
        return remote(e2s, e2r.at[y], e2_s.at[o], e2_r.at[o], peer * ZS + z, head)

    def e3_copy(o):
        peer = (z + o) % ZS
        rows = pl.ds(pl.multiple_of(z * PIECE, PIECE), PIECE)
        return remote(e3s.at[peer], inc.at[rows, :], e3_s.at[o], e3_r.at[o], y * ZS + peer, head)

    causal = row_id <= lane_id
    gains = [jnp.broadcast_to(gain_ref[h * HD : (h + 1) * HD].reshape(1, HD), (BLK, HD)).T for h in range(NH)]

    def mix_within(h):
        def some(g, carry):
            done = []
            for u in range(4):
                n = 4 * g + u
                at = pl.multiple_of(n * BLK, BLK)
                rowb = jnp.broadcast_to(cum_ref[n, h : h + 1, :], (BLK, BLK))
                gap = jnp.where(causal, rowb - rowb.T, HIDDEN)
                query = silu(lq[pl.ds(at, BLK), h * HD : (h + 1) * HD])
                scores = dot(kb[h, pl.ds(at, BLK), :], query, 1, 1)
                weights = (scores * jnp.exp(gap)).astype(BF16)
                done.append((at, query, dot(vraw[h, :, pl.ds(at, BLK)], weights)))
            for at, query, mixed in done:
                lq[pl.ds(at, BLK), h * HD : (h + 1) * HD] = query
                within[h, :, pl.ds(at, BLK)] = mixed
            return carry

        lax.fori_loop(0, NBL // 4, some, 0)

    for o in range(1, ZS):
        e1_copy(o).start()
    start_regroup(1)
    start_regroup(2)
    queries_here(0)
    hop1(0).start()
    hop1(1).start()
    e1r[z] = e1s[z]
    loads[2].wait()
    mix_within(0)

    def spread(mask, wide):
        for b in range(NBL):
            wide[:, b * BLK : (b + 1) * BLK] = jnp.broadcast_to(mask[:, b : b + 1], (NBL, BLK))

    for o in range(1, ZS):
        e1_copy(o).wait_recv()
    place = z * PIECE + lax.broadcasted_iota(jnp.int32, (PIECE, HD), 0)
    acc = jnp.zeros((PIECE, HD), F32)
    reach = jnp.ones((PIECE, HD), F32)
    before, reaches = [], []
    for s in range(ZS):
        before.append(acc)
        reaches.append(reach)
        tail = e1r[s, PIECE:, :].astype(F32)
        d = [tail[h : h + 1] + tail[8 + h : 9 + h] for h in range(NH)]
        step = jnp.where(place < HD, d[0], jnp.where(place < 2 * HD, d[1], d[2]))
        acc = step * acc + e1r[s, :PIECE, :].astype(F32)
        reach = reach * step
    e2s[:PIECE, :] = acc
    e2s[PIECE:, :] = reach
    for o in range(1, YS):
        e2_copy(o).start()
    hop1(2).start()
    mask_hop1.wait_recv()
    mask_hop2.start()
    e2r[y] = e2s[...]
    mix_within(1)
    for o in range(1, YS):
        e2_copy(o).wait_recv()
    offset = jnp.zeros((PIECE, HD), F32)
    for s in range(YS):
        new = e2r[s, PIECE:, :] * offset + e2r[s, :PIECE, :]
        offset = jnp.where(s < y, new, offset)
    for s in range(ZS):
        e3s[s] = (before[s] + reaches[s] * offset).astype(BF16)
    for o in range(1, ZS):
        e3_copy(o).start()
    start_hop2(0)
    start_hop2(1)
    hop1(3).start()
    inc[pl.ds(pl.multiple_of(z * PIECE, PIECE), PIECE), :] = e3s[z]

    def mix_head(h):
        def mix(g, state):
            done = []
            for u in range(UNROLL):
                n = UNROLL * g + u
                at = pl.multiple_of(n * BLK, BLK)
                row = cum_ref[n, h : h + 1, :]
                high = state.astype(BF16)
                low = (state - high.astype(F32)).astype(BF16)
                query = lq[pl.ds(at, BLK), h * HD : (h + 1) * HD]
                products = dot(jnp.concatenate([high, low], axis=0), query, 1, 1)
                mixed = within[h, :, pl.ds(at, BLK)] + jnp.exp(row) * (products[:HD] + products[HD:])
                square = jnp.mean(mixed * mixed, axis=0, keepdims=True)
                normed = (mixed * lax.rsqrt(square + EPSILON) * gains[h]).astype(BF16)
                state = jnp.exp(row[:, BLK - 1 :]) * state + upd[h, n]
                done.append((at, normed))
            for at, normed in done:
                vt[h, :, pl.ds(at, BLK)] = normed
                lin[pl.ds(at, BLK), h * HD : (h + 1) * HD] = normed.T
            return state

        lax.fori_loop(0, NBL // UNROLL, mix, inc[h * HD : (h + 1) * HD, :].astype(F32))
        store_lin(h).start()

    def store_lin(h):
        cols = slice(h * HD, (h + 1) * HD)
        return pltpu.make_async_copy(lin.at[:, cols], lin_any.at[:, cols], fin_sem.at[h])

    pair_row = lax.broadcasted_iota(jnp.int32, (BLK, PAIR), 0)
    pair_lane = lax.broadcasted_iota(jnp.int32, (BLK, PAIR), 1)

    def score(h, queries, bias, role, p):
        lanes = slice(p * PAIR, (p + 1) * PAIR)
        lo, hi = ((0, 2 * p + 2), (0, NBL), (2 * p, NBL))[role]
        logits = dot(kk[h, lo * BLK : hi * BLK, :], queries(p), 1, 1)
        parts = [logits[j * BLK : (j + 1) * BLK, :] for j in range(hi - lo)]
        if role == 0:
            for u in range(2):
                parts[u - 2] = jnp.where(pair_row + u * BLK <= pair_lane, parts[u - 2], HIDDEN)
        pens = [bias[lo + j : lo + j + 1, lanes] for j in range(hi - lo)]
        top = jnp.full((1, PAIR), FLOOR, F32)
        for part, pen in zip(parts, pens):
            top = jnp.maximum(top, jnp.max(part, axis=0, keepdims=True) * SCALE + pen)
        return lo, hi, parts, pens, top

    def weigh(h, lo, hi, parts, pens, top):
        weights = []
        total = jnp.zeros((8, PAIR), F32)
        for part, pen in zip(parts, pens):
            w = jnp.exp2(part * SCALE + (pen - top))
            total = total + jnp.sum(w.reshape(BLK // 8, 8, PAIR), axis=0)
            weights.append(w.astype(BF16))
        acc = dot(vt[h, :, lo * BLK : hi * BLK], jnp.concatenate(weights, axis=0))
        return jnp.sum(total, axis=0, keepdims=True), acc

    def attend(work):
        waiting = []

        def finish():
            c, u, out, stats, held = waiting.pop(0)
            l, acc = weigh(ORDER[c][0], *held)
            out[c, :, u * PAIR : (u + 1) * PAIR] = acc.astype(out.dtype)
            stats[c, u : u + 1, :] = held[-1]
            stats[c, PPP + u : PPP + u + 1, :] = l

        for c, queries, bias, role, out, stats in work:
            h, q = ORDER[c]
            for u in range(PPP):
                waiting.append((c, u, out, stats, score(h, queries, bias, role, q * PPP + u)))
                if len(waiting) > 1:
                    finish()
        finish()

    def merged(c, u, own, own_stats, part, stats):
        lanes = slice(u * PAIR, (u + 1) * PAIR)
        m, l = own_stats[c, u : u + 1, :], own_stats[c, PPP + u : PPP + u + 1, :]
        m_in, l_in = stats[c, u : u + 1, :], stats[c, PPP + u : PPP + u + 1, :]
        new = jnp.maximum(m, m_in)
        mine, theirs = jnp.exp2(m - new), jnp.exp2(m_in - new)
        acc = own[c, :, lanes] * mine + part[c, :, lanes].astype(F32) * theirs
        return new, l * mine + l_in * theirs, acc

    def forward(h, role):
        o_s, o_r, s_s, s_r = (o2s, o2r, s2s, s2r) if role == 2 else (o1s, o1r, s1s, s1r)
        return (
            remote(o_s.at[h], o_r.at[h], res_s.at[role, 0, h], res_r.at[role, 0, h], nxt, head),
            remote(s_s.at[h], s_r.at[h], res_s.at[role, 1, h], res_r.at[role, 1, h], nxt, head),
        )

    def out_region(h, sender):
        return soft_any.at[:, pl.ds(pl.multiple_of(sender * WIDTH + h * HD, HD), HD)]

    def out_copy(h, p, sender):
        rows = ost.at[h, pl.ds(p * SUB, SUB), :]
        return remote(rows, out_region(h, sender), out_s.at[h, p], out_r.at[h, sender], ctx, p)

    def out_own(h, p):
        return pltpu.make_async_copy(ost.at[h, pl.ds(p * SUB, SUB), :], out_region(h, head), fin_sem.at[NH + h])

    def far(c):
        hop2(c).wait_recv()
        attend([(c, lambda p: q2[c, (p % PPP) * PAIR : (p % PPP + 1) * PAIR, :], b2, 2, o2s, s2s)])
        for d in forward(c, 2):
            d.start()

    def near_and_own(c):
        attend([
            (c, lambda p: q1[c, (p % PPP) * PAIR : (p % PPP + 1) * PAIR, :], b1, 1, acc1, st1),
            (c, lambda p: q0[ORDER[c][0], p * PAIR : (p + 1) * PAIR, :], b0, 0, acc0, st0),
        ])

    def merge_near(c):
        for d in forward(c, 2):
            d.wait_recv()
        for u in range(PPP):
            m, l, acc = merged(c, u, acc1, st1, o2r, s2r)
            o1s[c, :, u * PAIR : (u + 1) * PAIR] = acc.astype(BF16)
            s1s[c, u : u + 1, :] = m
            s1s[c, PPP + u : PPP + u + 1, :] = l
        for d in forward(c, 1):
            d.start()

    def merge_own(c):
        for d in forward(c, 1):
            d.wait_recv()
        h = ORDER[c][0]
        for u in range(PPP):
            p = ORDER[c][1] * PPP + u
            m, l, acc = merged(c, u, acc0, st0, o1r, s1r)
            ost[h, p * PAIR : (p + 1) * PAIR, :] = (acc * (1.0 / l)).T.astype(BF16)

            @pl.when(head == p)
            def _():
                out_own(h, p).start()

            @pl.when(head != p)
            def _():
                out_copy(h, p, head).start()

    def keys_here(h):
        own_part(sk_any, kk, h, own_sem.at[1, h]).wait()
        for o in order:
            regroup(sk_any, kk, h, o, ks_sem, kr_sem).wait_recv()

    spread(near_mask[0], b1)
    mask_hop2.wait_recv()
    spread(far_mask[...], b2)
    mix_within(2)
    for o in range(1, ZS):
        e3_copy(o).wait_recv()
    mix_head(0)
    for c in range(PARTS):
        if c + 2 < PARTS:
            start_hop2(c + 2)
        if c + 4 < PARTS:
            if (c + 4) % SPLIT == 0:
                queries_here((c + 4) // SPLIT)
            hop1(c + 4).start()
        if c % SPLIT == 0:
            keys_here(c // SPLIT)
        far(c)
        near_and_own(c)
        if c >= 1:
            merge_near(c - 1)
        if c >= 2:
            merge_own(c - 2)
        if c in (1, 4):
            mix_head(1 if c == 1 else 2)
    merge_near(PARTS - 1)
    merge_own(PARTS - 2)
    merge_own(PARTS - 1)

    for h in range(NH):
        store_lin(h).wait()
        for o in order:
            regroup(sq_any, q0, h, o, qs_sem, qr_sem).wait_send()
            regroup(sk_any, kk, h, o, ks_sem, kr_sem).wait_send()
        for p in range(HEADS):

            @pl.when(head == p)
            def _():
                out_own(h, p).wait()

            @pl.when(head != p)
            def _():
                out_copy(h, p, head).wait_send()
                out_copy(h, p, p).wait_recv()
    for c in range(PARTS):
        hop1(c).wait_send()
        hop2(c).wait_send()
        for role in (1, 2):
            for d in forward(c, role):
                d.wait_send()
    mask_hop1.wait_send()
    mask_hop2.wait_send()
    for o in range(1, ZS):
        e1_copy(o).wait_send()
        e3_copy(o).wait_send()
    for o in range(1, YS):
        e2_copy(o).wait_send()


def hand_on(lin_in, soft_in, lin_out, soft_out, sem):
    copies = []
    for i in range(8):
        a, b = pl.ds(i * TOK // 8, TOK // 8), pl.ds(i * SUB // 8, SUB // 8)
        copies.append(pltpu.make_async_copy(lin_in.at[a, :], lin_out.at[a, :], sem.at[0, i]))
        copies.append(pltpu.make_async_copy(soft_in.at[b, :], soft_out.at[b, :], sem.at[1, i]))
    for c in copies:
        c.start()
    for c in copies:
        c.wait()


def shards(lin_query, lin_key, lin_value, log_decay, norm_gain, soft_query, soft_key, block_list):
    anywhere = pl.BlockSpec(memory_space=pl.ANY)
    vmem = pl.BlockSpec(memory_space=pltpu.VMEM)
    smem = pl.BlockSpec(memory_space=pltpu.SMEM)
    dma = pltpu.SemaphoreType.DMA
    wide = (NH, HD, TOK)
    part = (PARTS, HD, QUARTER)
    rows = (NH, TOK, HD)
    stats = (PARTS, 2 * PPP, PAIR)
    outs = (
        jax.ShapeDtypeStruct((TOK, WIDTH), BF16),
        jax.ShapeDtypeStruct((SUB, HEADS * WIDTH), BF16),
    )
    lin_out, soft_out = pl.pallas_call(
        body,
        out_shape=outs,
        in_specs=[anywhere, anywhere, anywhere, vmem, vmem, anywhere, anywhere, smem],
        out_specs=(anywhere, anywhere),
        scratch_shapes=[
            pltpu.VMEM((TOK, WIDTH), BF16),
            pltpu.VMEM((TOK, WIDTH), BF16),
            pltpu.VMEM((TOK, WIDTH), BF16),
            pltpu.VMEM(rows, BF16),
            pltpu.VMEM(wide, BF16),
            pltpu.VMEM((NBL, 8, BLK), F32),
            pltpu.VMEM((NH, NBL, HD, HD), F32),
            pltpu.VMEM((WIDTH, HD), F32),
            pltpu.VMEM(wide, F32),
            pltpu.VMEM((TOK, WIDTH), BF16),
            pltpu.VMEM(wide, BF16),
            pltpu.VMEM(part, F32),
            pltpu.VMEM(part, F32),
            pltpu.VMEM(stats, F32),
            pltpu.VMEM(stats, F32),
            pltpu.VMEM((NBL, TOK), F32),
            pltpu.VMEM((2, NBL, BLK), F32),
            pltpu.VMEM(rows, BF16),
            pltpu.VMEM((PARTS, QUARTER, HD), BF16),
            pltpu.VMEM((PARTS, QUARTER, HD), BF16),
            pltpu.VMEM(rows, BF16),
            pltpu.VMEM((NBL, TOK), F32),
            pltpu.VMEM((NBL, TOK), F32),
            pltpu.VMEM((NBL, BLK), F32),
            pltpu.VMEM((2, NBL, BLK), F32),
            pltpu.VMEM(part, BF16),
            pltpu.VMEM(part, BF16),
            pltpu.VMEM(part, BF16),
            pltpu.VMEM(part, BF16),
            pltpu.VMEM(stats, F32),
            pltpu.VMEM(stats, F32),
            pltpu.VMEM(stats, F32),
            pltpu.VMEM(stats, F32),
            pltpu.VMEM(rows, BF16),
            pltpu.VMEM((ZS, PIECE + 16, HD), BF16),
            pltpu.VMEM((ZS, PIECE + 16, HD), BF16),
            pltpu.VMEM((YS, 2 * PIECE, HD), F32),
            pltpu.VMEM((2 * PIECE, HD), F32),
            pltpu.VMEM((ZS, PIECE, HD), BF16),
            pltpu.VMEM((WIDTH, HD), BF16),
            dma((3,)),
            dma((2, NH)),
            dma((NH, HEADS)),
            dma((NH, HEADS)),
            dma((NH, HEADS)),
            dma((NH, HEADS)),
            dma((2, PARTS)),
            dma((2, PARTS)),
            dma((2,)),
            dma((2,)),
            dma((3, 2, PARTS)),
            dma((3, 2, PARTS)),
            dma((ZS,)),
            dma((ZS,)),
            dma((YS,)),
            dma((YS,)),
            dma((ZS,)),
            dma((ZS,)),
            dma((NH, HEADS)),
            dma((NH, HEADS)),
            dma((2 * NH,)),
        ],
        compiler_params=pltpu.CompilerParams(
            collective_id=0, has_side_effects=True, vmem_limit_bytes=56 * 1024 * 1024
        ),
        cost_estimate=pl.CostEstimate(flops=20_000_000_000, bytes_accessed=12_000_000, transcendentals=30_000_000),
    )(
        lin_query, lin_key, lin_value, log_decay, norm_gain, soft_query, soft_key, block_list
    )
    return pl.pallas_call(
        hand_on,
        out_shape=outs,
        in_specs=[anywhere, anywhere],
        out_specs=(anywhere, anywhere),
        scratch_shapes=[dma((2, 8))],
        cost_estimate=pl.CostEstimate(flops=0, bytes_accessed=6_300_000, transcendentals=0),
    )(lin_out, soft_out)


def solution(mesh):
    placed = (
        P("ctx", "head"),
        P("ctx", "head"),
        P("ctx", "head"),
        P("head", "ctx"),
        P("head"),
        P(("ctx", "head"), None),
        P(("ctx", "head"), None),
        P("ctx", None),
    )
    return jax.shard_map(
        shards,
        mesh=mesh,
        in_specs=placed,
        out_specs=(P("ctx", "head"), P(("ctx", "head"), None)),
        check_vma=False,
    )
```

```python
import functools
import math

import jax
import jax.numpy as jnp
from jax import lax
from jax.experimental import pallas as pl
from jax.experimental.pallas import tpu as pltpu
from jax.sharding import PartitionSpec as P

HD = 128
BLK = 128
NB = 16
EPSILON = 1e-06
UNROLL = 8
MESH = pl.DeviceIdType.MESH
F32 = jnp.float32
BF16 = jnp.bfloat16
SCALE = HD ** (-0.5) * math.log2(math.e)
HIDDEN = -1e30
FLOOR = -1e20

NH = 3
HEADS = 8
ZS, YS = 8, 4
NCTX = ZS * YS
TOK = 2048
NBL = TOK // BLK
SUB = TOK // HEADS
WIDTH = NH * HD
PIECE = WIDTH // ZS
PAIR = 2 * BLK
NPAIR = TOK // PAIR
SPLIT = 4
QUARTER = TOK // SPLIT
PPP = NPAIR // SPLIT
ORDER = [(h, q) for h in range(NH) for q in (range(SPLIT) if h == NH - 1 else range(SPLIT - 1, -1, -1))]
PARTS = len(ORDER)


def dot(a, b, ca=1, cb=0):
    return lax.dot_general(a, b, (((ca,), (cb,)), ((), ())), preferred_element_type=F32)


def silu(x):
    v = x.astype(F32)
    return (v / (1.0 + jnp.exp(-v))).astype(BF16)


def body(
    lq_any, lk_any, lv_any, decay_ref, gain_ref, sq_any, sk_any, list_ref,
    lin_any, soft_any,
    lq, lk, lv, kb, vraw, cum_ref, upd, state, within, lin, vt, acc0, acc1, st0, st1, b0, own_mask,
    q0, q1, q2, kk, b1, b2, far_mask, near_mask,
    o2s, o1s, o2r, o1r, s2s, s1s, s2r, s1r, ost,
    e1s, e1r, e2r, e2s, e3s, inc,
    load_sem, own_sem, qs_sem, qr_sem, ks_sem, kr_sem, hop_s, hop_r, bias_s, bias_r,
    res_s, res_r, e1_s, e1_r, e2_s, e2_r, e3_s, e3_r, out_s, out_r, fin_sem,
):
    ctx = lax.axis_index("ctx")
    head = lax.axis_index("head")
    y, z = ctx // ZS, ctx % ZS
    prev = (ctx + NCTX - 1) % NCTX
    nxt = (ctx + 1) % NCTX

    def remote(src, dst, ss, rs, c, h):
        return pltpu.make_async_remote_copy(
            src_ref=src, dst_ref=dst, send_sem=ss, recv_sem=rs, device_id=(c, h), device_id_type=MESH
        )

    loads = [
        pltpu.make_async_copy(lk_any, lk, load_sem.at[0]),
        pltpu.make_async_copy(lv_any, lv, load_sem.at[1]),
        pltpu.make_async_copy(lq_any, lq, load_sem.at[2]),
    ]
    for c in loads:
        c.start()

    barrier = pltpu.get_barrier_semaphore()
    greeted = 0
    for o in range(1, HEADS):
        pl.semaphore_signal(barrier, inc=1, device_id=(ctx, (head + o) % HEADS), device_id_type=MESH)
        greeted += 1
    for o in range(1, ZS):
        pl.semaphore_signal(barrier, inc=1, device_id=(y * ZS + (z + o) % ZS, head), device_id_type=MESH)
        greeted += 1
    for o in range(1, YS):
        pl.semaphore_signal(barrier, inc=1, device_id=(((y + o) % YS) * ZS + z, head), device_id_type=MESH)
        greeted += 1
    for c in (prev, nxt):
        pl.semaphore_signal(barrier, inc=1, device_id=(c, head), device_id_type=MESH)
        greeted += 1

    cum_ref[...] = jnp.zeros_like(cum_ref)
    for n in range(NBL):
        cum_ref[n, :NH, :] = decay_ref[:, n * BLK : (n + 1) * BLK]
    row_id = lax.broadcasted_iota(jnp.int32, (BLK, BLK), 0)
    lane_id = lax.broadcasted_iota(jnp.int32, (BLK, BLK), 1)
    until = (row_id <= lane_id).astype(F32).astype(BF16)
    rest = cum_ref[...].reshape(NBL * 8, BLK)
    total = jnp.zeros((NBL * 8, BLK), F32)
    for _ in range(3):
        part = rest.astype(BF16)
        total = total + dot(part, until)
        rest = rest - part.astype(F32)
    cum_ref[...] = total.reshape(NBL, 8, BLK)

    block_id = lax.broadcasted_iota(jnp.int32, (NBL, BLK), 0)
    block_lane = lax.broadcasted_iota(jnp.int32, (NBL, BLK), 1)
    for role in range(3):
        ids = block_id + (ctx - role) * NBL
        compact = jnp.full((NBL, BLK), HIDDEN, F32)
        for b in range(NBL):
            found = ids == list_ref[b, 0]
            for j in range(1, NB):
                found = found | (ids == list_ref[b, j])
            pen = jnp.where(found & (ids >= 0), 0.0, HIDDEN)
            if role == 0:
                b0[:, b * BLK : (b + 1) * BLK] = pen
            else:
                compact = jnp.where(block_lane == b, pen, compact)
        if role:
            own_mask[role - 1] = compact
    pl.semaphore_wait(barrier, greeted)

    def regroup(src, dst, h, o, ss, rs):
        peer = (head + o) % HEADS
        col = pl.multiple_of(peer * WIDTH + h * HD, HD)
        row = pl.multiple_of(head * SUB, SUB)
        return remote(src.at[:, pl.ds(col, HD)], dst.at[h, pl.ds(row, SUB), :], ss.at[h, o], rs.at[h, o], ctx, peer)

    def own_part(src, dst, h, sem):
        col = pl.multiple_of(head * WIDTH + h * HD, HD)
        row = pl.multiple_of(head * SUB, SUB)
        return pltpu.make_async_copy(src.at[:, pl.ds(col, HD)], dst.at[h, pl.ds(row, SUB), :], sem)

    order = (1, 7, 2, 6, 3, 5, 4)
    def start_regroup(h):
        own_part(sq_any, q0, h, own_sem.at[0, h]).start()
        for o in order:
            regroup(sq_any, q0, h, o, qs_sem, qr_sem).start()
        own_part(sk_any, kk, h, own_sem.at[1, h]).start()
        for o in order:
            regroup(sk_any, kk, h, o, ks_sem, kr_sem).start()

    start_regroup(0)
    mask_hop1 = remote(own_mask, near_mask, bias_s.at[0], bias_r.at[0], prev, head)
    mask_hop2 = remote(near_mask.at[1], far_mask, bias_s.at[1], bias_r.at[1], prev, head)

    def hop1(c):
        h, q = ORDER[c]
        return remote(q0.at[h, pl.ds(q * QUARTER, QUARTER), :], q1.at[c], hop_s.at[0, c], hop_r.at[0, c], prev, head)

    def hop2(c):
        return remote(q1.at[c], q2.at[c], hop_s.at[1, c], hop_r.at[1, c], prev, head)

    def queries_here(h):
        own_part(sq_any, q0, h, own_sem.at[0, h]).wait()
        for o in order:
            regroup(sq_any, q0, h, o, qs_sem, qr_sem).wait_recv()

    def start_hop2(c):
        hop1(c).wait_recv()
        hop2(c).start()

    mask_hop1.start()

    loads[0].wait()
    loads[1].wait()

    def gather_state(g, states):
        states = list(states)
        done = []
        for u in range(2):
            n = 2 * g + u
            at = pl.multiple_of(n * BLK, BLK)
            for h in range(NH):
                row = cum_ref[n, h : h + 1, :]
                end = row[:, BLK - 1 :]
                key = silu(lk[pl.ds(at, BLK), h * HD : (h + 1) * HD])
                value = lv[pl.ds(at, BLK), h * HD : (h + 1) * HD].T
                weighted = value.astype(F32) * jnp.exp(end - row)
                high = weighted.astype(BF16)
                low = (weighted - high.astype(F32)).astype(BF16)
                both = dot(jnp.concatenate([high, low], axis=0), key)
                update = both[:HD] + both[HD:]
                states[h] = jnp.exp(end) * states[h] + update
                done.append((h, n, at, key, value, update))
        for h, n, at, key, value, update in done:
            kb[h, pl.ds(at, BLK), :] = key
            vraw[h, :, pl.ds(at, BLK)] = value
            upd[h, n] = update
        return tuple(states)

    states = lax.fori_loop(0, NBL // 2, gather_state, tuple(jnp.zeros((HD, HD), F32) for _ in range(NH)))
    for h in range(NH):
        state[h * HD : (h + 1) * HD, :] = states[h]

    everything = jnp.sum(cum_ref[...], axis=0)[:, BLK - 1 :]
    decays = jnp.broadcast_to(jnp.exp(everything), (8, HD))
    coarse = decays.astype(BF16).astype(F32)
    tail = jnp.concatenate([coarse, decays - coarse], axis=0).astype(BF16)
    for p in range(ZS):
        e1s[p, :PIECE, :] = state[p * PIECE : (p + 1) * PIECE, :].astype(BF16)
        e1s[p, PIECE:, :] = tail

    def e1_copy(o):
        peer = (z + o) % ZS
        return remote(e1s.at[peer], e1r.at[z], e1_s.at[o], e1_r.at[o], y * ZS + peer, head)

    def e2_copy(o):
        peer = (y + o) % YS
        return remote(e2s, e2r.at[y], e2_s.at[o], e2_r.at[o], peer * ZS + z, head)

    def e3_copy(o):
        peer = (z + o) % ZS
        rows = pl.ds(pl.multiple_of(z * PIECE, PIECE), PIECE)
        return remote(e3s.at[peer], inc.at[rows, :], e3_s.at[o], e3_r.at[o], y * ZS + peer, head)

    causal = row_id <= lane_id
    gains = [jnp.broadcast_to(gain_ref[h * HD : (h + 1) * HD].reshape(1, HD), (BLK, HD)).T for h in range(NH)]

    def mix_within(h):
        def some(g, carry):
            done = []
            for u in range(4):
                n = 4 * g + u
                at = pl.multiple_of(n * BLK, BLK)
                rowb = jnp.broadcast_to(cum_ref[n, h : h + 1, :], (BLK, BLK))
                gap = jnp.where(causal, rowb - rowb.T, HIDDEN)
                query = silu(lq[pl.ds(at, BLK), h * HD : (h + 1) * HD])
                scores = dot(kb[h, pl.ds(at, BLK), :], query, 1, 1)
                weights = (scores * jnp.exp(gap)).astype(BF16)
                done.append((at, query, dot(vraw[h, :, pl.ds(at, BLK)], weights)))
            for at, query, mixed in done:
                lq[pl.ds(at, BLK), h * HD : (h + 1) * HD] = query
                within[h, :, pl.ds(at, BLK)] = mixed
            return carry

        lax.fori_loop(0, NBL // 4, some, 0)

    for o in range(1, ZS):
        e1_copy(o).start()
    start_regroup(1)
    start_regroup(2)
    queries_here(0)
    hop1(0).start()
    hop1(1).start()
    e1r[z] = e1s[z]
    loads[2].wait()
    mix_within(0)

    def spread(mask, wide):
        for b in range(NBL):
            wide[:, b * BLK : (b + 1) * BLK] = jnp.broadcast_to(mask[:, b : b + 1], (NBL, BLK))

    for o in range(1, ZS):
        e1_copy(o).wait_recv()
    place = z * PIECE + lax.broadcasted_iota(jnp.int32, (PIECE, HD), 0)
    acc = jnp.zeros((PIECE, HD), F32)
    reach = jnp.ones((PIECE, HD), F32)
    before, reaches = [], []
    for s in range(ZS):
        before.append(acc)
        reaches.append(reach)
        tail = e1r[s, PIECE:, :].astype(F32)
        d = [tail[h : h + 1] + tail[8 + h : 9 + h] for h in range(NH)]
        step = jnp.where(place < HD, d[0], jnp.where(place < 2 * HD, d[1], d[2]))
        acc = step * acc + e1r[s, :PIECE, :].astype(F32)
        reach = reach * step
    e2s[:PIECE, :] = acc
    e2s[PIECE:, :] = reach
    for o in range(1, YS):
        e2_copy(o).start()
    hop1(2).start()
    mask_hop1.wait_recv()
    mask_hop2.start()
    e2r[y] = e2s[...]
    for o in range(1, YS):
        e2_copy(o).wait_recv()
    offset = jnp.zeros((PIECE, HD), F32)
    for s in range(YS):
        new = e2r[s, PIECE:, :] * offset + e2r[s, :PIECE, :]
        offset = jnp.where(s < y, new, offset)
    for s in range(ZS):
        e3s[s] = (before[s] + reaches[s] * offset).astype(BF16)
    for o in range(1, ZS):
        e3_copy(o).start()
    for c in range(3):
        start_hop2(c)
    hop1(3).start()
    inc[pl.ds(pl.multiple_of(z * PIECE, PIECE), PIECE), :] = e3s[z]

    def mix_head(h):
        def mix(g, state):
            done = []
            for u in range(UNROLL):
                n = UNROLL * g + u
                at = pl.multiple_of(n * BLK, BLK)
                row = cum_ref[n, h : h + 1, :]
                high = state.astype(BF16)
                low = (state - high.astype(F32)).astype(BF16)
                query = lq[pl.ds(at, BLK), h * HD : (h + 1) * HD]
                products = dot(jnp.concatenate([high, low], axis=0), query, 1, 1)
                mixed = within[h, :, pl.ds(at, BLK)] + jnp.exp(row) * (products[:HD] + products[HD:])
                square = jnp.mean(mixed * mixed, axis=0, keepdims=True)
                normed = (mixed * lax.rsqrt(square + EPSILON) * gains[h]).astype(BF16)
                state = jnp.exp(row[:, BLK - 1 :]) * state + upd[h, n]
                done.append((at, normed))
            for at, normed in done:
                vt[h, :, pl.ds(at, BLK)] = normed
                lin[pl.ds(at, BLK), h * HD : (h + 1) * HD] = normed.T
            return state

        lax.fori_loop(0, NBL // UNROLL, mix, inc[h * HD : (h + 1) * HD, :].astype(F32))
        store_lin(h).start()

    def store_lin(h):
        cols = slice(h * HD, (h + 1) * HD)
        return pltpu.make_async_copy(lin.at[:, cols], lin_any.at[:, cols], fin_sem.at[h])

    pair_row = lax.broadcasted_iota(jnp.int32, (BLK, PAIR), 0)
    pair_lane = lax.broadcasted_iota(jnp.int32, (BLK, PAIR), 1)

    def score(h, queries, bias, role, p):
        lanes = slice(p * PAIR, (p + 1) * PAIR)
        lo, hi = ((0, 2 * p + 2), (0, NBL), (2 * p, NBL))[role]
        logits = dot(kk[h, lo * BLK : hi * BLK, :], queries(p), 1, 1)
        parts = [logits[j * BLK : (j + 1) * BLK, :] for j in range(hi - lo)]
        if role == 0:
            for u in range(2):
                parts[u - 2] = jnp.where(pair_row + u * BLK <= pair_lane, parts[u - 2], HIDDEN)
        pens = [bias[lo + j : lo + j + 1, lanes] for j in range(hi - lo)]
        top = jnp.full((1, PAIR), FLOOR, F32)
        for part, pen in zip(parts, pens):
            top = jnp.maximum(top, jnp.max(part, axis=0, keepdims=True) * SCALE + pen)
        return lo, hi, parts, pens, top

    def weigh(h, lo, hi, parts, pens, top):
        weights = []
        total = jnp.zeros((8, PAIR), F32)
        for part, pen in zip(parts, pens):
            w = jnp.exp2(part * SCALE + (pen - top))
            total = total + jnp.sum(w.reshape(BLK // 8, 8, PAIR), axis=0)
            weights.append(w.astype(BF16))
        acc = dot(vt[h, :, lo * BLK : hi * BLK], jnp.concatenate(weights, axis=0))
        return jnp.sum(total, axis=0, keepdims=True), acc

    def attend(work):
        waiting = []

        def finish():
            c, u, out, stats, held = waiting.pop(0)
            l, acc = weigh(ORDER[c][0], *held)
            out[c, :, u * PAIR : (u + 1) * PAIR] = acc.astype(out.dtype)
            stats[c, u : u + 1, :] = held[-1]
            stats[c, PPP + u : PPP + u + 1, :] = l

        for c, queries, bias, role, out, stats in work:
            h, q = ORDER[c]
            for u in range(PPP):
                waiting.append((c, u, out, stats, score(h, queries, bias, role, q * PPP + u)))
                if len(waiting) > 1:
                    finish()
        finish()

    def merged(c, u, own, own_stats, part, stats):
        lanes = slice(u * PAIR, (u + 1) * PAIR)
        m, l = own_stats[c, u : u + 1, :], own_stats[c, PPP + u : PPP + u + 1, :]
        m_in, l_in = stats[c, u : u + 1, :], stats[c, PPP + u : PPP + u + 1, :]
        new = jnp.maximum(m, m_in)
        mine, theirs = jnp.exp2(m - new), jnp.exp2(m_in - new)
        acc = own[c, :, lanes] * mine + part[c, :, lanes].astype(F32) * theirs
        return new, l * mine + l_in * theirs, acc

    def forward(h, role):
        o_s, o_r, s_s, s_r = (o2s, o2r, s2s, s2r) if role == 2 else (o1s, o1r, s1s, s1r)
        return (
            remote(o_s.at[h], o_r.at[h], res_s.at[role, 0, h], res_r.at[role, 0, h], nxt, head),
            remote(s_s.at[h], s_r.at[h], res_s.at[role, 1, h], res_r.at[role, 1, h], nxt, head),
        )

    def out_region(h, sender):
        return soft_any.at[:, pl.ds(pl.multiple_of(sender * WIDTH + h * HD, HD), HD)]

    def out_copy(h, p, sender):
        rows = ost.at[h, pl.ds(p * SUB, SUB), :]
        return remote(rows, out_region(h, sender), out_s.at[h, p], out_r.at[h, sender], ctx, p)

    def out_own(h, p):
        return pltpu.make_async_copy(ost.at[h, pl.ds(p * SUB, SUB), :], out_region(h, head), fin_sem.at[NH + h])

    def far(c):
        hop2(c).wait_recv()
        attend([(c, lambda p: q2[c, (p % PPP) * PAIR : (p % PPP + 1) * PAIR, :], b2, 2, o2s, s2s)])
        for d in forward(c, 2):
            d.start()

    def near(c):
        attend([(c, lambda p: q1[c, (p % PPP) * PAIR : (p % PPP + 1) * PAIR, :], b1, 1, acc1, st1)])

    def own(c):
        attend([(c, lambda p: q0[ORDER[c][0], p * PAIR : (p + 1) * PAIR, :], b0, 0, acc0, st0)])

    def merge_near(c):
        for d in forward(c, 2):
            d.wait_recv()
        for u in range(PPP):
            m, l, acc = merged(c, u, acc1, st1, o2r, s2r)
            o1s[c, :, u * PAIR : (u + 1) * PAIR] = acc.astype(BF16)
            s1s[c, u : u + 1, :] = m
            s1s[c, PPP + u : PPP + u + 1, :] = l
        for d in forward(c, 1):
            d.start()

    def merge_own(c):
        for d in forward(c, 1):
            d.wait_recv()
        h = ORDER[c][0]
        for u in range(PPP):
            p = ORDER[c][1] * PPP + u
            m, l, acc = merged(c, u, acc0, st0, o1r, s1r)
            ost[h, p * PAIR : (p + 1) * PAIR, :] = (acc * (1.0 / l)).T.astype(BF16)

            @pl.when(head == p)
            def _():
                out_own(h, p).start()

            @pl.when(head != p)
            def _():
                out_copy(h, p, head).start()

    def keys_here(h):
        own_part(sk_any, kk, h, own_sem.at[1, h]).wait()
        for o in order:
            regroup(sk_any, kk, h, o, ks_sem, kr_sem).wait_recv()

    spread(near_mask[0], b1)
    mask_hop2.wait_recv()
    spread(far_mask[...], b2)
    for o in range(1, ZS):
        e3_copy(o).wait_recv()
    mix_head(0)
    keys_here(0)
    far(0)
    queries_here(1)
    hop1(4).start()
    for c in range(PARTS):
        if c + 1 < PARTS:
            if (c + 1) % SPLIT == 0:
                keys_here((c + 1) // SPLIT)
            far(c + 1)
        near(c)
        merge_near(c)
        own(c)
        if c + 3 < PARTS:
            start_hop2(c + 3)
        if c + 5 < PARTS:
            if (c + 5) % SPLIT == 0:
                queries_here((c + 5) // SPLIT)
            hop1(c + 5).start()
        if c >= 1:
            merge_own(c - 1)
        if c in (1, 4):
            mix_within(1 if c == 1 else 2)
            mix_head(1 if c == 1 else 2)
    merge_own(PARTS - 1)

    for h in range(NH):
        store_lin(h).wait()
        for o in order:
            regroup(sq_any, q0, h, o, qs_sem, qr_sem).wait_send()
            regroup(sk_any, kk, h, o, ks_sem, kr_sem).wait_send()
        for p in range(HEADS):

            @pl.when(head == p)
            def _():
                out_own(h, p).wait()

            @pl.when(head != p)
            def _():
                out_copy(h, p, head).wait_send()
                out_copy(h, p, p).wait_recv()
    for c in range(PARTS):
        hop1(c).wait_send()
        hop2(c).wait_send()
        for role in (1, 2):
            for d in forward(c, role):
                d.wait_send()
    mask_hop1.wait_send()
    mask_hop2.wait_send()
    for o in range(1, ZS):
        e1_copy(o).wait_send()
        e3_copy(o).wait_send()
    for o in range(1, YS):
        e2_copy(o).wait_send()


def shards(lin_query, lin_key, lin_value, log_decay, norm_gain, soft_query, soft_key, block_list):
    anywhere = pl.BlockSpec(memory_space=pl.ANY)
    vmem = pl.BlockSpec(memory_space=pltpu.VMEM)
    smem = pl.BlockSpec(memory_space=pltpu.SMEM)
    dma = pltpu.SemaphoreType.DMA
    wide = (NH, HD, TOK)
    part = (PARTS, HD, QUARTER)
    rows = (NH, TOK, HD)
    stats = (PARTS, 2 * PPP, PAIR)
    outs = (
        jax.ShapeDtypeStruct((TOK, WIDTH), BF16),
        jax.ShapeDtypeStruct((SUB, HEADS * WIDTH), BF16),
    )
    return pl.pallas_call(
        body,
        out_shape=outs,
        in_specs=[anywhere, anywhere, anywhere, vmem, vmem, anywhere, anywhere, smem],
        out_specs=(anywhere, anywhere),
        scratch_shapes=[
            pltpu.VMEM((TOK, WIDTH), BF16),
            pltpu.VMEM((TOK, WIDTH), BF16),
            pltpu.VMEM((TOK, WIDTH), BF16),
            pltpu.VMEM(rows, BF16),
            pltpu.VMEM(wide, BF16),
            pltpu.VMEM((NBL, 8, BLK), F32),
            pltpu.VMEM((NH, NBL, HD, HD), F32),
            pltpu.VMEM((WIDTH, HD), F32),
            pltpu.VMEM(wide, F32),
            pltpu.VMEM((TOK, WIDTH), BF16),
            pltpu.VMEM(wide, BF16),
            pltpu.VMEM(part, F32),
            pltpu.VMEM(part, F32),
            pltpu.VMEM(stats, F32),
            pltpu.VMEM(stats, F32),
            pltpu.VMEM((NBL, TOK), F32),
            pltpu.VMEM((2, NBL, BLK), F32),
            pltpu.VMEM(rows, BF16),
            pltpu.VMEM((PARTS, QUARTER, HD), BF16),
            pltpu.VMEM((PARTS, QUARTER, HD), BF16),
            pltpu.VMEM(rows, BF16),
            pltpu.VMEM((NBL, TOK), F32),
            pltpu.VMEM((NBL, TOK), F32),
            pltpu.VMEM((NBL, BLK), F32),
            pltpu.VMEM((2, NBL, BLK), F32),
            pltpu.VMEM(part, BF16),
            pltpu.VMEM(part, BF16),
            pltpu.VMEM(part, BF16),
            pltpu.VMEM(part, BF16),
            pltpu.VMEM(stats, F32),
            pltpu.VMEM(stats, F32),
            pltpu.VMEM(stats, F32),
            pltpu.VMEM(stats, F32),
            pltpu.VMEM(rows, BF16),
            pltpu.VMEM((ZS, PIECE + 16, HD), BF16),
            pltpu.VMEM((ZS, PIECE + 16, HD), BF16),
            pltpu.VMEM((YS, 2 * PIECE, HD), F32),
            pltpu.VMEM((2 * PIECE, HD), F32),
            pltpu.VMEM((ZS, PIECE, HD), BF16),
            pltpu.VMEM((WIDTH, HD), BF16),
            dma((3,)),
            dma((2, NH)),
            dma((NH, HEADS)),
            dma((NH, HEADS)),
            dma((NH, HEADS)),
            dma((NH, HEADS)),
            dma((2, PARTS)),
            dma((2, PARTS)),
            dma((2,)),
            dma((2,)),
            dma((3, 2, PARTS)),
            dma((3, 2, PARTS)),
            dma((ZS,)),
            dma((ZS,)),
            dma((YS,)),
            dma((YS,)),
            dma((ZS,)),
            dma((ZS,)),
            dma((NH, HEADS)),
            dma((NH, HEADS)),
            dma((2 * NH,)),
        ],
        compiler_params=pltpu.CompilerParams(
            collective_id=0, has_side_effects=True, vmem_limit_bytes=56 * 1024 * 1024
        ),
        cost_estimate=pl.CostEstimate(flops=20_000_000_000, bytes_accessed=12_000_000, transcendentals=30_000_000),
    )(
        lin_query, lin_key, lin_value, log_decay, norm_gain, soft_query, soft_key, block_list
    )


def solution(mesh):
    placed = (
        P("ctx", "head"),
        P("ctx", "head"),
        P("ctx", "head"),
        P("head", "ctx"),
        P("head"),
        P(("ctx", "head"), None),
        P(("ctx", "head"), None),
        P("ctx", None),
    )
    return jax.shard_map(
        shards,
        mesh=mesh,
        in_specs=placed,
        out_specs=(P("ctx", "head"), P(("ctx", "head"), None)),
        check_vma=False,
    )
```
